32 devices in a mesh: groups: 1, frames: 32 (over z, y, x, core).
Axes of the slice: x: 2, y: 2, z: 4, core: 2. Of those that a mesh axis runs over, the one named last changes fastest.
Arguments:
- skip: bfloat16 [32, 256, 640], P(('groups', 'frames')), may hold values from -24 to 24
- control: bfloat16 [32, 256, 640], P('groups', 'frames'), may hold values from -6 to 6
- zero_weight: bfloat16 [640, 640], replicated, may hold values from -1 to 1
- gn_gain: float32 [640], replicated, may hold values from 0.1 to 1.9
- gn_bias: float32 [640], replicated, may hold values from -0.5 to 0.5
- conv_weight: bfloat16 [9, 640, 640], replicated, may hold values from -0.078125 to 0.078125
- ln_gain: float32 [640], replicated, may hold values from 0.1 to 1.9
- qkv_weight: bfloat16 [640, 1920], replicated, may hold values from -5 to 5
- out_weight: bfloat16 [640, 640], replicated, may hold values from -0.25 to 0.25
Outputs:
- output: bfloat16 [32, 256, 640], P(('groups', 'frames'))
The draws below stay inside these ranges and needn't reach their ends.
All inputs are finite; a program needn't handle non-finite values.
Results may differ from the reference program's by a relative error of at most 0.0043.
Values may be sent and summed in bfloat16 or wider, within the bound.
A program may use at most 64 MiB of HBM per device.

```python
import math
import jax
import jax.numpy as jnp
from jax import lax

C = 640
HEADS = 10
HD = 64
GROUPS = 32
CLIP = 32
H = 8
W = 32
FRAMES = 32
PIX = 256


def shared_jitter(key):
    jitter = jax.random.uniform(jax.random.fold_in(key, 101), (FRAMES, GROUPS), jnp.float32, -4.0, 4.0)
    return jnp.repeat(jitter, C // GROUPS, axis=1)[:, None, :]


def draw_skip(key, part):
    first_key = jax.random.fold_in(jax.random.fold_in(key, 11), 0)
    fourth_key = jax.random.fold_in(jax.random.fold_in(key, 11), 3)
    fifth_key = jax.random.fold_in(jax.random.fold_in(key, 11), 4)
    frame_pos = (jnp.arange(FRAMES) % CLIP).astype(jnp.float32)
    ramp = (1.0 + 2.0 * frame_pos / (CLIP - 1))[:, None, None]
    magnitude = jax.random.uniform(fourth_key, (GROUPS,), jnp.float32, 0.75, 1.75)
    flips = jnp.where(jax.random.uniform(fifth_key, (GROUPS,), jnp.float32) > 0.5, 1.0, -1.0)
    offset = jnp.repeat(magnitude * flips, C // GROUPS)[None, None, :]
    jitter = shared_jitter(key)
    values = (jnp.clip(jax.random.normal(first_key, (FRAMES, PIX, C), jnp.float32), -6.0, 6.0) + offset) * ramp + jitter
    return jnp.clip(values, -24.0, 24.0).astype(jnp.bfloat16)


def draw_control(key, part):
    first_key, second_key = jax.random.split(jax.random.fold_in(key, 37), 2)
    coupling = jax.random.uniform(first_key, (GROUPS,), jnp.float32, 0.6, 1.4)
    coupling = jnp.repeat(coupling, C // GROUPS)[None, None, :]
    jitter = shared_jitter(key)
    noise = jnp.clip(jax.random.normal(second_key, (FRAMES, PIX, C), jnp.float32), -4.0, 4.0)
    return jnp.clip(coupling * jitter + noise, -6.0, 6.0).astype(jnp.bfloat16)


def draw_zero_weight(key, part):
    noise = jnp.clip(jax.random.normal(jax.random.fold_in(key, 53), (C, C), jnp.float32), -4.0, 4.0)
    values = 0.75 * jnp.eye(C, dtype=jnp.float32) + 0.7 * C ** (-0.5) * noise
    return jnp.clip(values, -1.0, 1.0).astype(jnp.bfloat16)


def draw_qkv_weight(key, part):
    noise = jnp.clip(jax.random.normal(jax.random.fold_in(key, 23), (C, 3 * C), jnp.float32), -6.0, 6.0) * C ** (-0.5)
    return jnp.clip(noise, -5.0, 5.0).astype(jnp.bfloat16)


def normal_values(key, dims, spread, reach, kind=jnp.bfloat16):
    array = spread * jax.random.normal(key, dims, jnp.float32)
    return jnp.clip(array, min=-reach, max=reach).astype(kind)


def setup_inputs(seed: int = 0, part: int = 0) -> dict:
    key_of = jax.random.split(jax.random.key(seed), 10)
    own_keys = jax.random.split(jax.random.fold_in(key_of[9], part), 10)
    skip = draw_skip(jax.random.fold_in(jax.random.fold_in(key_of[9], part), 71), part)
    control = draw_control(jax.random.fold_in(jax.random.fold_in(key_of[9], part), 71), part)
    zero_weight = draw_zero_weight(jax.random.fold_in(key_of[9], 71), part)
    gn_gain = jnp.clip(1.0 + 0.18 * jax.random.normal(key_of[3], (C,), jnp.float32), 0.1, 1.9)
    gn_bias = jnp.clip(jax.random.uniform(key_of[4], (C,), jnp.float32, -0.5, 0.5), -0.5, 0.5)
    conv_weight = normal_values(key_of[5], (9, C, C), (9 * C) ** -0.5, 0.078125)
    ln_gain = jnp.clip(1.0 + 0.18 * jax.random.normal(key_of[6], (C,), jnp.float32), 0.1, 1.9)
    qkv_weight = draw_qkv_weight(jax.random.fold_in(key_of[9], 71), part)
    out_weight = normal_values(key_of[8], (C, C), C ** -0.5, 0.25)
    return {"skip": skip, "control": control, "zero_weight": zero_weight, "gn_gain": gn_gain, "gn_bias": gn_bias, "conv_weight": conv_weight, "ln_gain": ln_gain, "qkv_weight": qkv_weight, "out_weight": out_weight}


norm_epsilon = 1e-05

def attend_all(qkv_rows):
    frame_count, pixel_count, _ = qkv_rows.shape
    clip_count = frame_count // CLIP
    shaped = qkv_rows.astype(jnp.float32).reshape(clip_count, CLIP, pixel_count, 3, HEADS, HD)
    queries = shaped[:, :, :, 0]
    key_rows = shaped[:, :, :, 1]
    value_rows = shaped[:, :, :, 2]
    scores = jnp.einsum('atphd,asphd->aphts', queries, key_rows, precision=lax.Precision.HIGHEST) * (1.0 / math.sqrt(HD))
    scores = scores - lax.optimization_barrier(jnp.max(scores, axis=-1, keepdims=True))
    expon = jnp.exp(scores)
    attn_weights = (expon / lax.optimization_barrier(jnp.sum(expon, axis=-1, keepdims=True))).astype(jnp.bfloat16)
    mixed = jnp.einsum('aphts,asphd->atphd', attn_weights.astype(jnp.float32), value_rows, precision=lax.Precision.HIGHEST)
    return mixed.astype(jnp.bfloat16).reshape(frame_count, pixel_count, C)

def reference(skip, control, zero_weight, gn_gain, gn_bias, conv_weight, ln_gain, qkv_weight, out_weight):
    zero_out = jnp.dot(control.reshape(-1, C), zero_weight, preferred_element_type=jnp.float32).astype(jnp.bfloat16)
    joined = skip.astype(jnp.float32) + zero_out.reshape(FRAMES, PIX, C).astype(jnp.float32)
    grouped = joined.reshape(FRAMES // CLIP, CLIP, PIX, GROUPS, C // GROUPS)
    clip_mean = lax.optimization_barrier(jnp.mean(grouped, axis=(1, 2, 4), keepdims=True))
    clip_var = lax.optimization_barrier(jnp.mean(jnp.square(grouped - clip_mean), axis=(1, 2, 4), keepdims=True))
    normed_groups = ((grouped - clip_mean) * lax.rsqrt(clip_var + norm_epsilon)).reshape(FRAMES, PIX, C)
    activated = jax.nn.silu(normed_groups * gn_gain + gn_bias).astype(jnp.bfloat16).reshape(FRAMES, H, W, C)
    padded = jnp.pad(activated, ((0, 0), (1, 1), (1, 1), (0, 0)))
    conv_sum = jnp.zeros((FRAMES * PIX, C), jnp.float32)
    for tap_index in range(9):
        row_shift, col_shift = divmod(tap_index, 3)
        window = padded[:, row_shift:row_shift + H, col_shift:col_shift + W, :].reshape(-1, C)
        conv_sum = conv_sum + jnp.dot(window, conv_weight[tap_index], preferred_element_type=jnp.float32)
    resid = joined.reshape(-1, C) + conv_sum
    token_mean = lax.optimization_barrier(jnp.mean(resid, axis=-1, keepdims=True))
    token_var = lax.optimization_barrier(jnp.mean(jnp.square(resid - token_mean), axis=-1, keepdims=True))
    normed = ((resid - token_mean) * lax.rsqrt(token_var + norm_epsilon) * ln_gain).astype(jnp.bfloat16)
    qkv_rows = jnp.dot(normed, qkv_weight, preferred_element_type=jnp.float32).astype(jnp.bfloat16)
    attended = attend_all(qkv_rows.reshape(FRAMES, PIX, 3 * C))
    output = resid + jnp.dot(attended.reshape(-1, C), out_weight, preferred_element_type=jnp.float32)
    return output.astype(jnp.bfloat16).reshape(FRAMES, PIX, C)
```

```python
import functools
import math

import jax
import jax.numpy as jnp
from jax import lax
from jax.experimental import pallas as pl
from jax.experimental.pallas import tpu as pltpu
from jax.sharding import PartitionSpec as P

HEADS = 10
HD = 64
GROUPS = 32
CLIP = 32
W = 32
LANES = 128
EPS = 1e-05
MESH = pl.DeviceIdType.MESH
HIGH = lax.Precision.HIGHEST
F32 = jnp.float32
BF16 = jnp.bfloat16


def kernel(
    n, fused_entry,
    skip_hbm, entry_hbm, zero_hbm, gain_ref, bias_ref, conv_hbm, ln_ref, qkv_hbm, wout_hbm,
    out_ref,
    skip_ref, entry_ref, zero_ref, conv_ref, qkv_ref, wout_ref,
    zero_send, zero_recv, joined, stat_send, stat_recv, window, norm_send, norm_recv,
    att_send, att_recv, load_sem, send_sem, recv_sem,
):
    me = lax.axis_index("frames")
    rows, chans = skip_ref.shape
    base = me // CLIP * CLIP
    spot = lax.rem(me, CLIP)

    loads = [
        pltpu.make_async_copy(src, dst, load_sem.at[i])
        for i, (src, dst) in enumerate([
            (entry_hbm, entry_ref), (zero_hbm, zero_ref), (skip_hbm, skip_ref),
            (conv_hbm, conv_ref), (qkv_hbm, qkv_ref), (wout_hbm, wout_ref),
        ])
    ]
    for load in loads:
        load.start()

    barrier = pltpu.get_barrier_semaphore()
    first, count, mine = (0, n, me) if fused_entry else (base, CLIP, spot)

    def greet(step, carry):
        pl.semaphore_signal(
            barrier, inc=1, device_id={"frames": first + lax.rem(mine + step, count)},
            device_id_type=MESH,
        )
        return carry

    lax.fori_loop(1, count, greet, 0)

    def exchange(phase, origin, total, place, pick, recv):
        def push(step, carry):
            other = lax.rem(place + step, total)
            pltpu.make_async_remote_copy(
                src_ref=pick(other), dst_ref=recv.at[place],
                send_sem=send_sem.at[phase], recv_sem=recv_sem.at[phase],
                device_id={"frames": origin + other}, device_id_type=MESH,
            ).start()
            return carry

        lax.fori_loop(1, total, push, 0)

    def arrive(phase, total, recv):
        part = recv.at[pl.ds(0, total - 1)]
        pltpu.make_async_copy(part, part, recv_sem.at[phase]).wait()

    def leave(phase, total, recv):
        part = recv.at[pl.ds(0, total - 1)]
        pltpu.make_async_copy(part, part, send_sem.at[phase]).wait()

    def flat(value):
        return value.astype(F32).reshape(-1, value.shape[-1])

    loads[0].wait()
    loads[1].wait()
    if fused_entry:
        zero_out = jnp.dot(entry_ref[...], zero_ref[...], preferred_element_type=F32)
        zero_send[...] = zero_out.reshape(zero_send.shape).astype(BF16)
        zero_recv[me] = zero_send[me]
    pl.semaphore_wait(barrier, count - 1)
    if fused_entry:
        exchange(0, 0, n, me, lambda other: zero_send.at[other], zero_recv)

    width = chans // GROUPS
    members = (
        lax.broadcasted_iota(jnp.int32, (chans, LANES), 0) // width
        == lax.broadcasted_iota(jnp.int32, (chans, LANES), 1)
    ).astype(F32)
    members_t = (
        lax.broadcasted_iota(jnp.int32, (LANES, chans), 1) // width
        == lax.broadcasted_iota(jnp.int32, (LANES, chans), 0)
    ).astype(F32)
    window[:W, :] = jnp.zeros((W, window.shape[1]), BF16)
    window[rows + W:, :] = jnp.zeros((W, window.shape[1]), BF16)
    loads[2].wait()

    if fused_entry:
        arrive(0, n, zero_recv)
        entry = flat(zero_recv[...])
    else:
        entry = entry_ref[...].astype(F32)
    together = skip_ref[...].astype(F32) + entry
    joined[...] = together
    sums = jnp.sum(together, axis=0, keepdims=True)
    squares = jnp.sum(together * together, axis=0, keepdims=True)
    lead = lax.broadcasted_iota(jnp.int32, (8, chans), 0)
    both = jnp.where(lead == 0, sums, jnp.where(lead == 1, squares, 0.0))
    stat_send[...] = jnp.dot(both, members, preferred_element_type=F32, precision=HIGH)
    stat_recv[spot] = stat_send[...]
    exchange(1, base, CLIP, spot, lambda other: stat_send, stat_recv)
    arrive(1, CLIP, stat_recv)
    size = float(CLIP * rows * width)
    totals = jnp.sum(stat_recv[...], axis=0) / size
    group_mean = totals[0:1, :]
    group_var = totals[1:2, :] - group_mean * group_mean
    group_inv = lax.rsqrt(group_var + EPS)
    lead = lax.broadcasted_iota(jnp.int32, (8, LANES), 0)
    both = jnp.where(lead == 0, group_mean, jnp.where(lead == 1, group_inv, 0.0))
    spread = jnp.dot(both, members_t, preferred_element_type=F32, precision=HIGH)
    value = (joined[...] - spread[0:1, :]) * spread[1:2, :] * gain_ref[...] + bias_ref[...]
    active = value / (1.0 + jnp.exp(-value))
    active = active.astype(BF16).astype(F32)

    column = lax.rem(lax.broadcasted_iota(jnp.int32, (rows, chans), 0), W)
    body_rows = slice(W, rows + W)
    window[body_rows, 0:chans] = jnp.where(column == 0, 0.0, pltpu.roll(active, 1, 0)).astype(BF16)
    window[body_rows, chans:2 * chans] = active.astype(BF16)
    window[body_rows, 2 * chans:] = jnp.where(
        column == W - 1, 0.0, pltpu.roll(active, rows - 1, 0)
    ).astype(BF16)
    loads[3].wait()
    resid = joined[...]
    for tap in range(3):
        resid = resid + jnp.dot(
            window[tap * W:tap * W + rows, :], conv_ref[tap], preferred_element_type=F32
        )
    joined[...] = resid

    mean = jnp.mean(resid, axis=-1, keepdims=True)
    centred = resid - mean
    var = jnp.mean(centred * centred, axis=-1, keepdims=True)
    normed = centred * lax.rsqrt(var + EPS) * ln_ref[...]
    norm_send[...] = normed.reshape(norm_send.shape).astype(BF16)
    norm_recv[spot] = norm_send[spot]
    exchange(2, base, CLIP, spot, lambda other: norm_send.at[other], norm_recv)
    loads[4].wait()
    loads[5].wait()
    arrive(2, CLIP, norm_recv)

    pix = norm_send.shape[1]
    tokens = flat(norm_recv[...]).astype(BF16)
    qkv = jnp.dot(tokens, qkv_ref[...], preferred_element_type=F32).astype(BF16)
    same = (
        lax.rem(lax.broadcasted_iota(jnp.int32, (rows, rows), 0), pix)
        == lax.rem(lax.broadcasted_iota(jnp.int32, (rows, rows), 1), pix)
    )
    low = lax.broadcasted_iota(jnp.int32, (rows, LANES), 1) < HD
    scale = 1.0 / math.sqrt(HD)
    for pair in range(chans // LANES):
        lo = pair * LANES
        queries = qkv[:, lo:lo + LANES].astype(F32) * scale
        keys = qkv[:, chans + lo:chans + lo + LANES]
        values = qkv[:, 2 * chans + lo:2 * chans + lo + LANES]
        mixed = []
        for half in (low, jnp.logical_not(low)):
            scores = lax.dot_general(
                jnp.where(half, queries, 0.0).astype(BF16), keys, (((1,), (1,)), ((), ())),
                preferred_element_type=F32,
            )
            scores = jnp.where(same, scores, -jnp.inf)
            expon = jnp.exp(scores - jnp.max(scores, axis=-1, keepdims=True))
            weights = (expon / jnp.sum(expon, axis=-1, keepdims=True)).astype(BF16)
            mixed.append(jnp.dot(weights, values, preferred_element_type=F32))
        result = jnp.where(low, mixed[0], mixed[1])
        att_send[:, :, lo:lo + LANES] = result.reshape(CLIP, pix, LANES).astype(BF16)
    att_recv[spot] = att_send[spot]
    exchange(3, base, CLIP, spot, lambda other: att_send.at[other], att_recv)
    arrive(3, CLIP, att_recv)
    attended = flat(att_recv[...]).astype(BF16)
    out_ref[...] = (
        joined[...] + jnp.dot(attended, wout_ref[...], preferred_element_type=F32)
    ).astype(BF16)
    if fused_entry:
        leave(0, n, zero_recv)
    leave(1, CLIP, stat_recv)
    leave(2, CLIP, norm_recv)
    leave(3, CLIP, att_recv)


def body(
    skip, control, zero_weight, gn_gain, gn_bias, conv_weight, ln_gain, qkv_weight, out_weight
):
    f_dev, rows, chans = skip.shape
    n = lax.axis_size("frames")
    frames, pix_dev, _ = control.shape
    assert f_dev == 1 and n % CLIP == 0 and rows % CLIP == 0
    fused_entry = pix_dev % 8 == 0
    if fused_entry:
        entry = control.reshape(frames * pix_dev, chans)
        entry_block = (n, pix_dev, chans)
    else:
        zero_out = jnp.dot(
            control.reshape(-1, chans), zero_weight, preferred_element_type=F32
        ).astype(BF16).reshape(control.shape)
        entry = lax.all_to_all(
            zero_out, "frames", split_axis=0, concat_axis=1, tiled=True
        ).reshape(rows, chans)
        entry_block = (8, 8, LANES)
    pix = rows // CLIP
    block = (CLIP, pix, chans)
    any_spec = pl.BlockSpec(memory_space=pl.ANY)
    vmem_spec = pl.BlockSpec(memory_space=pltpu.VMEM)
    call = pl.pallas_call(
        functools.partial(kernel, n, fused_entry),
        out_shape=jax.ShapeDtypeStruct((rows, chans), BF16),
        in_specs=[
            any_spec, any_spec, any_spec, vmem_spec, vmem_spec, any_spec, vmem_spec,
            any_spec, any_spec,
        ],
        out_specs=vmem_spec,
        scratch_shapes=[
            pltpu.VMEM((rows, chans), BF16),
            pltpu.VMEM(entry.shape, BF16),
            pltpu.VMEM(zero_weight.shape, BF16),
            pltpu.VMEM((3, 3 * chans, chans), BF16),
            pltpu.VMEM(qkv_weight.shape, BF16),
            pltpu.VMEM(out_weight.shape, BF16),
            pltpu.VMEM(entry_block, BF16),
            pltpu.VMEM(entry_block, BF16),
            pltpu.VMEM((rows, chans), F32),
            pltpu.VMEM((8, LANES), F32),
            pltpu.VMEM((CLIP, 8, LANES), F32),
            pltpu.VMEM((rows + 2 * W, 3 * chans), BF16),
            pltpu.VMEM(block, BF16),
            pltpu.VMEM(block, BF16),
            pltpu.VMEM(block, BF16),
            pltpu.VMEM(block, BF16),
            pltpu.SemaphoreType.DMA((6,)),
            pltpu.SemaphoreType.DMA((4,)),
            pltpu.SemaphoreType.DMA((4,)),
        ],
        compiler_params=pltpu.CompilerParams(
            collective_id=0, has_side_effects=True, vmem_limit_bytes=48 * 1024 * 1024
        ),
    )
    out = call(
        skip.reshape(rows, chans), entry, zero_weight, gn_gain.reshape(1, chans),
        gn_bias.reshape(1, chans), conv_weight.reshape(3, 3 * chans, chans),
        ln_gain.reshape(1, chans), qkv_weight, out_weight,
    )
    return out.reshape(skip.shape)


def solution(mesh):
    frames = P(("groups", "frames"), None, None)
    return jax.shard_map(
        body, mesh=mesh,
        in_specs=(frames, P("groups", "frames", None), P(), P(), P(), P(), P(), P(), P()),
        out_specs=frames, check_vma=False,
    )
```

```python
import functools
import math

import jax
import jax.numpy as jnp
from jax import lax
from jax.experimental import pallas as pl
from jax.experimental.pallas import tpu as pltpu
from jax.sharding import PartitionSpec as P

HEADS = 10
HD = 64
GROUPS = 32
CLIP = 32
W = 32
LANES = 128
EPS = 1e-05
MESH = pl.DeviceIdType.MESH
F32 = jnp.float32
BF16 = jnp.bfloat16


def parts(row):
    top = row.astype(BF16).astype(F32)
    middle = (row - top).astype(BF16).astype(F32)
    return [top, middle, row - top - middle]


def pool(first, second, matrix):
    rows = parts(first) + parts(second)
    lead = lax.broadcasted_iota(jnp.int32, (16, first.shape[1]), 0)
    stack = jnp.zeros(lead.shape, F32)
    for i, row in enumerate(rows):
        stack = jnp.where(lead == i, row, stack)
    product = jnp.dot(stack.astype(BF16), matrix, preferred_element_type=F32)
    return (
        product[0:1] + product[1:2] + product[2:3],
        product[3:4] + product[4:5] + product[5:6],
    )


def kernel(
    n, fused_entry,
    skip_hbm, entry_hbm, zero_hbm, gain_hbm, bias_hbm, conv_hbm, ln_hbm, qkv_hbm, wout_hbm,
    out_ref,
    skip_ref, entry_ref, zero_ref, conv_ref, qkv_ref, wout_ref, gain_ref, bias_ref, ln_ref,
    zero_send, zero_recv, joined, stat_send, stat_recv, window, norm_send, norm_recv,
    att_send, att_recv, load_sem, send_sem, recv_sem,
):
    me = lax.axis_index("frames")
    rows, chans = skip_ref.shape
    base = me // CLIP * CLIP
    spot = lax.rem(me, CLIP)

    loads = [
        pltpu.make_async_copy(src, dst, load_sem.at[i])
        for i, (src, dst) in enumerate([
            (entry_hbm, entry_ref), (zero_hbm, zero_ref), (skip_hbm, skip_ref),
            (conv_hbm, conv_ref), (qkv_hbm, qkv_ref), (wout_hbm, wout_ref),
            (gain_hbm, gain_ref), (bias_hbm, bias_ref), (ln_hbm, ln_ref),
        ])
    ]
    for load in loads:
        load.start()

    barrier = pltpu.get_barrier_semaphore()
    first, count, mine = (0, n, me) if fused_entry else (base, CLIP, spot)

    def greet(step, carry):
        pl.semaphore_signal(
            barrier, inc=1, device_id={"frames": first + lax.rem(mine + step, count)},
            device_id_type=MESH,
        )
        return carry

    lax.fori_loop(1, count, greet, 0)

    def exchange(phase, origin, total, place, pick, recv):
        def push(step, carry):
            other = lax.rem(place + step, total)
            pltpu.make_async_remote_copy(
                src_ref=pick(other), dst_ref=recv.at[place],
                send_sem=send_sem.at[phase], recv_sem=recv_sem.at[phase],
                device_id={"frames": origin + other}, device_id_type=MESH,
            ).start()
            return carry

        lax.fori_loop(1, total, push, 0)

    def arrive(phase, total, recv):
        part = recv.at[pl.ds(0, total - 1)]
        pltpu.make_async_copy(part, part, recv_sem.at[phase]).wait()

    def leave(phase, total, recv):
        part = recv.at[pl.ds(0, total - 1)]
        pltpu.make_async_copy(part, part, send_sem.at[phase]).wait()

    def flat(value):
        return value.astype(F32).reshape(-1, value.shape[-1])

    loads[0].wait()
    loads[1].wait()
    if fused_entry:
        zero_out = jnp.dot(entry_ref[...], zero_ref[...], preferred_element_type=F32)
        zero_send[...] = zero_out.reshape(zero_send.shape).astype(BF16)
        zero_recv[me] = zero_send[me]
    pl.semaphore_wait(barrier, count - 1)
    if fused_entry:
        exchange(0, 0, n, me, lambda other: zero_send.at[other], zero_recv)

    width = chans // GROUPS
    members = (
        lax.broadcasted_iota(jnp.int32, (chans, LANES), 0) // width
        == lax.rem(lax.broadcasted_iota(jnp.int32, (chans, LANES), 1), GROUPS)
    ).astype(F32).astype(BF16)
    members_t = (
        lax.broadcasted_iota(jnp.int32, (LANES, chans), 1) // width
        == lax.rem(lax.broadcasted_iota(jnp.int32, (LANES, chans), 0), GROUPS)
    ).astype(F32).astype(BF16)
    window[:W, :] = jnp.zeros((W, window.shape[1]), BF16)
    window[rows + W:, :] = jnp.zeros((W, window.shape[1]), BF16)
    loads[2].wait()

    if fused_entry:
        arrive(0, n, zero_recv)
        entry = flat(zero_recv[...])
    else:
        entry = entry_ref[...].astype(F32)
    together = skip_ref[...].astype(F32) + entry
    joined[...] = together
    sums = jnp.sum(together, axis=0, keepdims=True)
    squares = jnp.sum(together * together, axis=0, keepdims=True)
    sums, squares = pool(sums, squares, members)
    lane = lax.broadcasted_iota(jnp.int32, (1, LANES), 1)
    stat_send[...] = jnp.where(lane < GROUPS, sums, squares)
    stat_recv[spot] = stat_send[...]
    exchange(1, base, CLIP, spot, lambda other: stat_send, stat_recv)
    arrive(1, CLIP, stat_recv)
    size = float(CLIP * rows * width)
    totals = jnp.sum(stat_recv[...], axis=0) / size
    group_mean, group_sq = pool(
        jnp.where(lane < GROUPS, totals, 0.0),
        jnp.where((lane >= GROUPS) & (lane < 2 * GROUPS), totals, 0.0),
        members_t,
    )
    group_inv = lax.rsqrt(group_sq - group_mean * group_mean + EPS)
    loads[6].wait()
    loads[7].wait()
    gain = gain_ref[...].reshape(1, chans)
    bias = bias_ref[...].reshape(1, chans)
    value = (joined[...] - group_mean) * group_inv * gain + bias
    active = value / (1.0 + jnp.exp(-value))
    active = active.astype(BF16).astype(F32)

    column = lax.rem(lax.broadcasted_iota(jnp.int32, (rows, chans), 0), W)
    body_rows = slice(W, rows + W)
    window[body_rows, 0:chans] = jnp.where(column == 0, 0.0, pltpu.roll(active, 1, 0)).astype(BF16)
    window[body_rows, chans:2 * chans] = active.astype(BF16)
    window[body_rows, 2 * chans:] = jnp.where(
        column == W - 1, 0.0, pltpu.roll(active, rows - 1, 0)
    ).astype(BF16)
    loads[3].wait()
    resid = joined[...]
    for tap in range(3):
        resid = resid + jnp.dot(
            window[tap * W:tap * W + rows, :], conv_ref[tap], preferred_element_type=F32
        )
    joined[...] = resid

    loads[8].wait()
    mean = jnp.mean(resid, axis=-1, keepdims=True)
    centred = resid - mean
    var = jnp.mean(centred * centred, axis=-1, keepdims=True)
    normed = centred * lax.rsqrt(var + EPS) * ln_ref[...].reshape(1, chans)
    norm_send[...] = normed.reshape(norm_send.shape).astype(BF16)
    norm_recv[spot] = norm_send[spot]
    exchange(2, base, CLIP, spot, lambda other: norm_send.at[other], norm_recv)
    loads[4].wait()
    loads[5].wait()
    arrive(2, CLIP, norm_recv)

    pix = norm_send.shape[1]
    tokens = flat(norm_recv[...]).astype(BF16)
    qkv = jnp.dot(tokens, qkv_ref[...], preferred_element_type=F32).astype(BF16)
    same = (
        lax.rem(lax.broadcasted_iota(jnp.int32, (rows, rows), 0), pix)
        == lax.rem(lax.broadcasted_iota(jnp.int32, (rows, rows), 1), pix)
    )
    low = lax.broadcasted_iota(jnp.int32, (rows, LANES), 1) < HD
    scale = 1.0 / math.sqrt(HD)
    for pair in range(chans // LANES):
        lo = pair * LANES
        queries = qkv[:, lo:lo + LANES].astype(F32) * scale
        keys = qkv[:, chans + lo:chans + lo + LANES]
        values = qkv[:, 2 * chans + lo:2 * chans + lo + LANES]
        mixed = []
        for half in (low, jnp.logical_not(low)):
            scores = lax.dot_general(
                jnp.where(half, queries, 0.0).astype(BF16), keys, (((1,), (1,)), ((), ())),
                preferred_element_type=F32,
            )
            scores = jnp.where(same, scores, -jnp.inf)
            expon = jnp.exp(scores - jnp.max(scores, axis=-1, keepdims=True))
            weights = (expon * (1.0 / jnp.sum(expon, axis=-1, keepdims=True))).astype(BF16)
            mixed.append(jnp.dot(weights, values, preferred_element_type=F32))
        result = jnp.where(low, mixed[0], mixed[1])
        att_send[:, :, lo:lo + LANES] = result.reshape(CLIP, pix, LANES).astype(BF16)
    att_recv[spot] = att_send[spot]
    exchange(3, base, CLIP, spot, lambda other: att_send.at[other], att_recv)
    arrive(3, CLIP, att_recv)
    attended = flat(att_recv[...]).astype(BF16)
    out_ref[...] = (
        joined[...] + jnp.dot(attended, wout_ref[...], preferred_element_type=F32)
    ).astype(BF16)
    if fused_entry:
        leave(0, n, zero_recv)
    leave(1, CLIP, stat_recv)
    leave(2, CLIP, norm_recv)
    leave(3, CLIP, att_recv)


def body(
    skip, control, zero_weight, gn_gain, gn_bias, conv_weight, ln_gain, qkv_weight, out_weight
):
    f_dev, rows, chans = skip.shape
    n = lax.axis_size("frames")
    frames, pix_dev, _ = control.shape
    assert f_dev == 1 and n % CLIP == 0 and rows % CLIP == 0
    fused_entry = pix_dev % 8 == 0
    if fused_entry:
        entry = control.reshape(frames * pix_dev, chans)
        entry_block = (n, pix_dev, chans)
    else:
        zero_out = jnp.dot(
            control.reshape(-1, chans), zero_weight, preferred_element_type=F32
        ).astype(BF16).reshape(control.shape)
        entry = lax.all_to_all(
            zero_out, "frames", split_axis=0, concat_axis=1, tiled=True
        ).reshape(rows, chans)
        entry_block = (8, 8, LANES)
    pix = rows // CLIP
    block = (CLIP, pix, chans)
    hbm_spec = pl.BlockSpec(memory_space=pltpu.HBM)
    vmem_spec = pl.BlockSpec(memory_space=pltpu.VMEM)
    call = pl.pallas_call(
        functools.partial(kernel, n, fused_entry),
        out_shape=jax.ShapeDtypeStruct((rows, chans), BF16),
        in_specs=[hbm_spec] * 9,
        out_specs=vmem_spec,
        scratch_shapes=[
            pltpu.VMEM((rows, chans), BF16),
            pltpu.VMEM(entry.shape, BF16),
            pltpu.VMEM(zero_weight.shape, BF16),
            pltpu.VMEM((3, 3 * chans, chans), BF16),
            pltpu.VMEM(qkv_weight.shape, BF16),
            pltpu.VMEM(out_weight.shape, BF16),
            pltpu.VMEM((chans,), F32),
            pltpu.VMEM((chans,), F32),
            pltpu.VMEM((chans,), F32),
            pltpu.VMEM(entry_block, BF16),
            pltpu.VMEM(entry_block, BF16),
            pltpu.VMEM((rows, chans), F32),
            pltpu.VMEM((1, LANES), F32),
            pltpu.VMEM((CLIP, 1, LANES), F32),
            pltpu.VMEM((rows + 2 * W, 3 * chans), BF16),
            pltpu.VMEM(block, BF16),
            pltpu.VMEM(block, BF16),
            pltpu.VMEM(block, BF16),
            pltpu.VMEM(block, BF16),
            pltpu.SemaphoreType.DMA((9,)),
            pltpu.SemaphoreType.DMA((4,)),
            pltpu.SemaphoreType.DMA((4,)),
        ],
        compiler_params=pltpu.CompilerParams(
            collective_id=0, has_side_effects=True, vmem_limit_bytes=60 * 1024 * 1024
        ),
    )
    out = call(
        skip.reshape(rows, chans), entry, zero_weight, gn_gain, gn_bias,
        conv_weight.reshape(3, 3 * chans, chans), ln_gain, qkv_weight, out_weight,
    )
    return out.reshape(skip.shape)


def solution(mesh):
    frames = P(("groups", "frames"), None, None)
    return jax.shard_map(
        body, mesh=mesh,
        in_specs=(frames, P("groups", "frames", None), P(), P(), P(), P(), P(), P(), P()),
        out_specs=frames, check_vma=False,
    )
```

```python
import functools
import math

import jax
import jax.numpy as jnp
from jax import lax
from jax.experimental import pallas as pl
from jax.experimental.pallas import tpu as pltpu
from jax.sharding import PartitionSpec as P

HEADS = 10
HD = 64
GROUPS = 32
CLIP = 32
W = 32
LANES = 128
HALVES = 2
EPS = 1e-05
MESH = pl.DeviceIdType.MESH
F32 = jnp.float32
BF16 = jnp.bfloat16


def parts(row):
    top = row.astype(BF16).astype(F32)
    middle = (row - top).astype(BF16).astype(F32)
    return [top, middle, row - top - middle]


def pool(first, second, matrix):
    rows = parts(first) + parts(second)
    lead = lax.broadcasted_iota(jnp.int32, (16, first.shape[1]), 0)
    stack = jnp.zeros(lead.shape, F32)
    for i, row in enumerate(rows):
        stack = jnp.where(lead == i, row, stack)
    product = jnp.dot(stack.astype(BF16), matrix, preferred_element_type=F32)
    return (
        product[0:1] + product[1:2] + product[2:3],
        product[3:4] + product[4:5] + product[5:6],
    )


def kernel(
    n, fused_entry,
    skip_hbm, entry_hbm, zero_hbm, gain_hbm, bias_hbm, conv_hbm, ln_hbm, qkv_hbm, wout_hbm,
    out_ref,
    skip_ref, entry_ref, zero_ref, conv_ref, qkv_ref, wout_ref, gain_ref, bias_ref, ln_ref,
    zero_send, zero_recv, joined, stat_send, stat_recv, window, norm_send, norm_recv,
    att_send, att_recv, load_sem, send_sem, recv_sem,
):
    me = lax.axis_index("frames")
    rows, chans = skip_ref.shape
    base = me // CLIP * CLIP
    spot = lax.rem(me, CLIP)
    per = CLIP // HALVES
    own_block = lax.rem(spot, HALVES) * per + spot // HALVES

    loads = [
        pltpu.make_async_copy(src, dst, load_sem.at[i])
        for i, (src, dst) in enumerate([
            (entry_hbm, entry_ref), (zero_hbm, zero_ref), (skip_hbm, skip_ref),
            (conv_hbm, conv_ref), (qkv_hbm, qkv_ref), (wout_hbm, wout_ref),
            (gain_hbm, gain_ref), (bias_hbm, bias_ref), (ln_hbm, ln_ref),
        ])
    ]
    for load in loads[:3]:
        load.start()

    barrier = pltpu.get_barrier_semaphore()
    first, count, mine = (0, n, me) if fused_entry else (base, CLIP, spot)

    def greet(step, carry):
        pl.semaphore_signal(
            barrier, inc=1, device_id={"frames": first + lax.rem(mine + step, count)},
            device_id_type=MESH,
        )
        return carry

    lax.fori_loop(1, count, greet, 0)

    def exchange(phase, origin, total, place, pick, recv, slot):
        def push(step, carry):
            other = lax.rem(place + step, total)
            pltpu.make_async_remote_copy(
                src_ref=pick(other), dst_ref=recv.at[slot],
                send_sem=send_sem.at[phase], recv_sem=recv_sem.at[phase],
                device_id={"frames": origin + other}, device_id_type=MESH,
            ).start()
            return carry

        lax.fori_loop(1, total, push, 0)

    def arrive(phase, total, recv):
        part = recv.at[pl.ds(0, total - 1)]
        pltpu.make_async_copy(part, part, recv_sem.at[phase]).wait()

    def leave(phase, total, recv):
        part = recv.at[pl.ds(0, total - 1)]
        pltpu.make_async_copy(part, part, send_sem.at[phase]).wait()

    def flat(value):
        return value.astype(F32).reshape(-1, value.shape[-1])

    loads[0].wait()
    loads[1].wait()
    for load in loads[3:]:
        load.start()
    if fused_entry:
        zero_out = jnp.dot(entry_ref[...], zero_ref[...], preferred_element_type=F32)
        zero_send[...] = zero_out.reshape(zero_send.shape).astype(BF16)
        zero_recv[me] = zero_send[me]
    pl.semaphore_wait(barrier, count - 1)
    if fused_entry:
        exchange(0, 0, n, me, lambda other: zero_send.at[other], zero_recv, me)

    width = chans // GROUPS
    members = (
        lax.broadcasted_iota(jnp.int32, (chans, LANES), 0) // width
        == lax.rem(lax.broadcasted_iota(jnp.int32, (chans, LANES), 1), GROUPS)
    ).astype(F32).astype(BF16)
    members_t = (
        lax.broadcasted_iota(jnp.int32, (LANES, chans), 1) // width
        == lax.rem(lax.broadcasted_iota(jnp.int32, (LANES, chans), 0), GROUPS)
    ).astype(F32).astype(BF16)
    window[:W, :] = jnp.zeros((W, window.shape[1]), BF16)
    window[rows + W:, :] = jnp.zeros((W, window.shape[1]), BF16)
    loads[2].wait()

    if fused_entry:
        arrive(0, n, zero_recv)
        entry = flat(zero_recv[...])
    else:
        entry = entry_ref[...].astype(F32)
    together = skip_ref[...].astype(F32) + entry
    joined[...] = together
    sums = jnp.sum(together, axis=0, keepdims=True)
    squares = jnp.sum(together * together, axis=0, keepdims=True)
    sums, squares = pool(sums, squares, members)
    lane = lax.broadcasted_iota(jnp.int32, (1, LANES), 1)
    stat_send[...] = jnp.where(lane < GROUPS, sums, squares)
    stat_recv[spot] = stat_send[...]
    exchange(1, base, CLIP, spot, lambda other: stat_send, stat_recv, spot)
    arrive(1, CLIP, stat_recv)
    size = float(CLIP * rows * width)
    totals = jnp.sum(stat_recv[...], axis=0) / size
    group_mean, group_sq = pool(
        jnp.where(lane < GROUPS, totals, 0.0),
        jnp.where((lane >= GROUPS) & (lane < 2 * GROUPS), totals, 0.0),
        members_t,
    )
    group_inv = lax.rsqrt(group_sq - group_mean * group_mean + EPS)
    loads[6].wait()
    loads[7].wait()
    gain = gain_ref[...].reshape(1, chans)
    bias = bias_ref[...].reshape(1, chans)
    value = (joined[...] - group_mean) * group_inv * gain + bias
    active = value / (1.0 + jnp.exp(-value))
    active = active.astype(BF16).astype(F32)

    column = lax.rem(lax.broadcasted_iota(jnp.int32, (rows, chans), 0), W)
    body_rows = slice(W, rows + W)
    window[body_rows, 0:chans] = jnp.where(column == 0, 0.0, pltpu.roll(active, 1, 0)).astype(BF16)
    window[body_rows, chans:2 * chans] = active.astype(BF16)
    window[body_rows, 2 * chans:] = jnp.where(
        column == W - 1, 0.0, pltpu.roll(active, rows - 1, 0)
    ).astype(BF16)
    loads[3].wait()
    loads[8].wait()
    ln_gain = ln_ref[...].reshape(1, chans)
    deep = rows // HALVES
    for half in range(HALVES):
        top = half * deep
        resid = joined[top:top + deep, :]
        for tap in range(3):
            start = top + tap * W
            resid = resid + jnp.dot(
                window[start:start + deep, :], conv_ref[tap], preferred_element_type=F32
            )
        joined[top:top + deep, :] = resid
        mean = jnp.mean(resid, axis=-1, keepdims=True)
        centred = resid - mean
        var = jnp.mean(centred * centred, axis=-1, keepdims=True)
        normed = centred * lax.rsqrt(var + EPS) * ln_gain
        norm_send[half * per:(half + 1) * per] = normed.reshape(
            (per,) + norm_send.shape[1:]
        ).astype(BF16)

        def push(step, carry, half=half):
            place = lax.rem(step + spot // HALVES, per)
            other = place * HALVES + half

            @pl.when(other != spot)
            def _():
                pltpu.make_async_remote_copy(
                    src_ref=norm_send.at[half * per + place], dst_ref=norm_recv.at[spot],
                    send_sem=send_sem.at[2], recv_sem=recv_sem.at[2],
                    device_id={"frames": base + other}, device_id_type=MESH,
                ).start()

            return carry

        lax.fori_loop(1, per + 1, push, 0)
    norm_recv[spot] = norm_send[own_block]
    loads[4].wait()
    loads[5].wait()
    arrive(2, CLIP, norm_recv)

    pix = norm_send.shape[1]
    tokens = flat(norm_recv[...]).astype(BF16)
    qkv = jnp.dot(tokens, qkv_ref[...], preferred_element_type=F32).astype(BF16)
    same = (
        lax.rem(lax.broadcasted_iota(jnp.int32, (rows, rows), 0), pix)
        == lax.rem(lax.broadcasted_iota(jnp.int32, (rows, rows), 1), pix)
    )
    low = lax.broadcasted_iota(jnp.int32, (rows, LANES), 1) < HD
    scale = 1.0 / math.sqrt(HD)
    for pair in range(chans // LANES):
        lo = pair * LANES
        queries = qkv[:, lo:lo + LANES].astype(F32) * scale
        keys = qkv[:, chans + lo:chans + lo + LANES]
        values = qkv[:, 2 * chans + lo:2 * chans + lo + LANES]
        mixed = []
        for half in (low, jnp.logical_not(low)):
            scores = lax.dot_general(
                jnp.where(half, queries, 0.0).astype(BF16), keys, (((1,), (1,)), ((), ())),
                preferred_element_type=F32,
            )
            scores = jnp.where(same, scores, -jnp.inf)
            expon = jnp.exp(scores - jnp.max(scores, axis=-1, keepdims=True))
            weights = (expon * (1.0 / jnp.sum(expon, axis=-1, keepdims=True))).astype(BF16)
            mixed.append(jnp.dot(weights, values, preferred_element_type=F32))
        result = jnp.where(low, mixed[0], mixed[1])
        att_send[:, :, lo:lo + LANES] = result.reshape(CLIP, pix, LANES).astype(BF16)
    att_recv[own_block] = att_send[spot]
    exchange(3, base, CLIP, spot, lambda other: att_send.at[other], att_recv, own_block)
    arrive(3, CLIP, att_recv)
    attended = flat(att_recv[...]).astype(BF16)
    out_ref[...] = (
        joined[...] + jnp.dot(attended, wout_ref[...], preferred_element_type=F32)
    ).astype(BF16)
    if fused_entry:
        leave(0, n, zero_recv)
    leave(1, CLIP, stat_recv)
    leave(2, CLIP, norm_recv)
    leave(3, CLIP, att_recv)


def body(
    skip, control, zero_weight, gn_gain, gn_bias, conv_weight, ln_gain, qkv_weight, out_weight
):
    f_dev, rows, chans = skip.shape
    n = lax.axis_size("frames")
    frames, pix_dev, _ = control.shape
    assert f_dev == 1 and n % CLIP == 0 and rows % CLIP == 0
    fused_entry = pix_dev % 8 == 0
    if fused_entry:
        entry = control.reshape(frames * pix_dev, chans)
        entry_block = (n, pix_dev, chans)
    else:
        zero_out = jnp.dot(
            control.reshape(-1, chans), zero_weight, preferred_element_type=F32
        ).astype(BF16).reshape(control.shape)
        entry = lax.all_to_all(
            zero_out, "frames", split_axis=0, concat_axis=1, tiled=True
        ).reshape(rows, chans)
        entry_block = (8, 8, LANES)
    pix = rows // CLIP
    block = (CLIP, pix, chans)
    hbm_spec = pl.BlockSpec(memory_space=pltpu.HBM)
    vmem_spec = pl.BlockSpec(memory_space=pltpu.VMEM)
    call = pl.pallas_call(
        functools.partial(kernel, n, fused_entry),
        out_shape=jax.ShapeDtypeStruct((rows, chans), BF16),
        in_specs=[hbm_spec] * 9,
        out_specs=vmem_spec,
        scratch_shapes=[
            pltpu.VMEM((rows, chans), BF16),
            pltpu.VMEM(entry.shape, BF16),
            pltpu.VMEM(zero_weight.shape, BF16),
            pltpu.VMEM((3, 3 * chans, chans), BF16),
            pltpu.VMEM(qkv_weight.shape, BF16),
            pltpu.VMEM(out_weight.shape, BF16),
            pltpu.VMEM((chans,), F32),
            pltpu.VMEM((chans,), F32),
            pltpu.VMEM((chans,), F32),
            pltpu.VMEM(entry_block, BF16),
            pltpu.VMEM(entry_block, BF16),
            pltpu.VMEM((rows, chans), F32),
            pltpu.VMEM((1, LANES), F32),
            pltpu.VMEM((CLIP, 1, LANES), F32),
            pltpu.VMEM((rows + 2 * W, 3 * chans), BF16),
            pltpu.VMEM(block, BF16),
            pltpu.VMEM(block, BF16),
            pltpu.VMEM(block, BF16),
            pltpu.VMEM(block, BF16),
            pltpu.SemaphoreType.DMA((9,)),
            pltpu.SemaphoreType.DMA((4,)),
            pltpu.SemaphoreType.DMA((4,)),
        ],
        compiler_params=pltpu.CompilerParams(
            collective_id=0, has_side_effects=True, vmem_limit_bytes=60 * 1024 * 1024
        ),
    )
    out = call(
        skip.reshape(rows, chans), entry, zero_weight, gn_gain, gn_bias,
        conv_weight.reshape(3, 3 * chans, chans), ln_gain, qkv_weight, out_weight,
    )
    return out.reshape(skip.shape)


def solution(mesh):
    frames = P(("groups", "frames"), None, None)
    return jax.shard_map(
        body, mesh=mesh,
        in_specs=(frames, P("groups", "frames", None), P(), P(), P(), P(), P(), P(), P()),
        out_specs=frames, check_vma=False,
    )
```

```python
import functools
import math

import jax
import jax.numpy as jnp
from jax import lax
from jax.experimental import pallas as pl
from jax.experimental.pallas import tpu as pltpu
from jax.sharding import PartitionSpec as P

HEADS = 10
HD = 64
GROUPS = 32
CLIP = 32
W = 32
LANES = 128
HALVES = 2
EPS = 1e-05
MESH = pl.DeviceIdType.MESH
F32 = jnp.float32
BF16 = jnp.bfloat16


def parts(row):
    top = row.astype(BF16).astype(F32)
    middle = (row - top).astype(BF16).astype(F32)
    return [top, middle, row - top - middle]


def pool(first, second, matrix):
    rows = parts(first) + parts(second)
    lead = lax.broadcasted_iota(jnp.int32, (16, first.shape[1]), 0)
    stack = jnp.zeros(lead.shape, F32)
    for i, row in enumerate(rows):
        stack = jnp.where(lead == i, row, stack)
    product = jnp.dot(stack.astype(BF16), matrix, preferred_element_type=F32)
    return (
        product[0:1] + product[1:2] + product[2:3],
        product[3:4] + product[4:5] + product[5:6],
    )


def kernel(
    n, fused_entry,
    skip_hbm, entry_hbm, zero_hbm, gain_hbm, bias_hbm, conv_hbm, ln_hbm, qkv_hbm, wout_hbm,
    out_ref,
    skip_ref, entry_ref, zero_ref, conv_ref, qkv_ref, wout_ref, gain_ref, bias_ref, ln_ref,
    zero_send, zero_recv, joined, stat_send, stat_recv, window, norm_send, norm_recv,
    att_send_a, att_send_b, att_recv_a, att_recv_b, load_sem, send_sem, recv_sem,
):
    me = lax.axis_index("frames")
    rows, chans = skip_ref.shape
    base = me // CLIP * CLIP
    spot = lax.rem(me, CLIP)
    per = CLIP // HALVES
    own_block = lax.rem(spot, HALVES) * per + spot // HALVES

    loads = [
        pltpu.make_async_copy(src, dst, load_sem.at[i])
        for i, (src, dst) in enumerate([
            (entry_hbm, entry_ref), (zero_hbm, zero_ref), (skip_hbm, skip_ref),
            (conv_hbm, conv_ref), (qkv_hbm, qkv_ref), (wout_hbm, wout_ref),
            (gain_hbm, gain_ref), (bias_hbm, bias_ref), (ln_hbm, ln_ref),
        ])
    ]
    for load in loads[:3]:
        load.start()

    barrier = pltpu.get_barrier_semaphore()
    first, count, mine = (0, n, me) if fused_entry else (base, CLIP, spot)

    def greet(step, carry):
        pl.semaphore_signal(
            barrier, inc=1, device_id={"frames": first + lax.rem(mine + step, count)},
            device_id_type=MESH,
        )
        return carry

    lax.fori_loop(1, count, greet, 0)

    def exchange(phase, origin, total, place, pick, recv, slot):
        def push(step, carry):
            other = lax.rem(place + step, total)

            @pl.when(other != place)
            def _():
                pltpu.make_async_remote_copy(
                    src_ref=pick(other), dst_ref=recv.at[slot],
                    send_sem=send_sem.at[phase], recv_sem=recv_sem.at[phase],
                    device_id={"frames": origin + other}, device_id_type=MESH,
                ).start()

            return carry

        lax.fori_loop(total // 4, total + total // 4, push, 0)

    def arrive(phase, total, recv):
        part = recv.at[pl.ds(0, total - 1)]
        pltpu.make_async_copy(part, part, recv_sem.at[phase]).wait()

    def leave(phase, total, recv):
        part = recv.at[pl.ds(0, total - 1)]
        pltpu.make_async_copy(part, part, send_sem.at[phase]).wait()

    def give_back(phase, source, recv):
        recv[own_block] = source[spot]
        exchange(phase, base, CLIP, spot, lambda other: source.at[other], recv, own_block)

    def flat(value):
        return value.astype(F32).reshape(-1, value.shape[-1])

    loads[0].wait()
    loads[1].wait()
    for load in loads[3:]:
        load.start()
    if fused_entry:
        zero_out = jnp.dot(entry_ref[...], zero_ref[...], preferred_element_type=F32)
        zero_send[...] = zero_out.reshape(zero_send.shape).astype(BF16)
        zero_recv[me] = zero_send[me]
    pl.semaphore_wait(barrier, count - 1)
    if fused_entry:
        exchange(0, 0, n, me, lambda other: zero_send.at[other], zero_recv, me)

    width = chans // GROUPS
    members = (
        lax.broadcasted_iota(jnp.int32, (chans, LANES), 0) // width
        == lax.rem(lax.broadcasted_iota(jnp.int32, (chans, LANES), 1), GROUPS)
    ).astype(F32).astype(BF16)
    members_t = (
        lax.broadcasted_iota(jnp.int32, (LANES, chans), 1) // width
        == lax.rem(lax.broadcasted_iota(jnp.int32, (LANES, chans), 0), GROUPS)
    ).astype(F32).astype(BF16)
    window[:W, :] = jnp.zeros((W, window.shape[1]), BF16)
    window[rows + W:, :] = jnp.zeros((W, window.shape[1]), BF16)
    loads[2].wait()

    if fused_entry:
        arrive(0, n, zero_recv)
        entry = flat(zero_recv[...])
    else:
        entry = entry_ref[...].astype(F32)
    together = skip_ref[...].astype(F32) + entry
    joined[...] = together
    sums = jnp.sum(together, axis=0, keepdims=True)
    squares = jnp.sum(together * together, axis=0, keepdims=True)
    sums, squares = pool(sums, squares, members)
    lane = lax.broadcasted_iota(jnp.int32, (1, LANES), 1)
    stat_send[...] = jnp.where(lane < GROUPS, sums, squares)
    stat_recv[spot] = stat_send[...]
    exchange(1, base, CLIP, spot, lambda other: stat_send, stat_recv, spot)
    arrive(1, CLIP, stat_recv)
    size = float(CLIP * rows * width)
    totals = jnp.sum(stat_recv[...], axis=0) / size
    group_mean, group_sq = pool(
        jnp.where(lane < GROUPS, totals, 0.0),
        jnp.where((lane >= GROUPS) & (lane < 2 * GROUPS), totals, 0.0),
        members_t,
    )
    group_inv = lax.rsqrt(group_sq - group_mean * group_mean + EPS)
    loads[6].wait()
    loads[7].wait()
    gain = gain_ref[...].reshape(1, chans)
    bias = bias_ref[...].reshape(1, chans)
    value = (joined[...] - group_mean) * group_inv * gain + bias
    active = value / (1.0 + jnp.exp(-value))
    active = active.astype(BF16).astype(F32)

    column = lax.rem(lax.broadcasted_iota(jnp.int32, (rows, chans), 0), W)
    body_rows = slice(W, rows + W)
    window[body_rows, 0:chans] = jnp.where(column == 0, 0.0, pltpu.roll(active, 1, 0)).astype(BF16)
    window[body_rows, chans:2 * chans] = active.astype(BF16)
    window[body_rows, 2 * chans:] = jnp.where(
        column == W - 1, 0.0, pltpu.roll(active, rows - 1, 0)
    ).astype(BF16)
    loads[3].wait()
    loads[8].wait()
    ln_gain = ln_ref[...].reshape(1, chans)
    deep = rows // HALVES
    for half in range(HALVES):
        top = half * deep
        resid = joined[top:top + deep, :]
        for tap in range(3):
            start = top + tap * W
            resid = resid + jnp.dot(
                window[start:start + deep, :], conv_ref[tap], preferred_element_type=F32
            )
        joined[top:top + deep, :] = resid
        mean = jnp.mean(resid, axis=-1, keepdims=True)
        centred = resid - mean
        var = jnp.mean(centred * centred, axis=-1, keepdims=True)
        normed = centred * lax.rsqrt(var + EPS) * ln_gain
        norm_send[half * per:(half + 1) * per] = normed.reshape(
            (per,) + norm_send.shape[1:]
        ).astype(BF16)

        def push(step, carry, half=half):
            place = lax.rem(step + spot // HALVES, per)
            other = place * HALVES + half

            @pl.when(other != spot)
            def _():
                pltpu.make_async_remote_copy(
                    src_ref=norm_send.at[half * per + place], dst_ref=norm_recv.at[spot],
                    send_sem=send_sem.at[2], recv_sem=recv_sem.at[2],
                    device_id={"frames": base + other}, device_id_type=MESH,
                ).start()

            return carry

        lax.fori_loop(per // 4, per + per // 4, push, 0)
    norm_recv[spot] = norm_send[own_block]
    loads[4].wait()
    loads[5].wait()
    arrive(2, CLIP, norm_recv)

    pix = norm_send.shape[1]
    tokens = flat(norm_recv[...]).astype(BF16)
    qkv = jnp.dot(tokens, qkv_ref[...], preferred_element_type=F32).astype(BF16)
    same = (
        lax.rem(lax.broadcasted_iota(jnp.int32, (rows, rows), 0), pix)
        == lax.rem(lax.broadcasted_iota(jnp.int32, (rows, rows), 1), pix)
    )
    low = lax.broadcasted_iota(jnp.int32, (rows, LANES), 1) < HD
    scale = 1.0 / math.sqrt(HD)
    split = att_send_a.shape[-1]
    for pair in range(chans // LANES):
        lo = pair * LANES
        att_send, col = (att_send_a, lo) if lo < split else (att_send_b, lo - split)
        queries = qkv[:, lo:lo + LANES].astype(F32) * scale
        keys = qkv[:, chans + lo:chans + lo + LANES]
        values = qkv[:, 2 * chans + lo:2 * chans + lo + LANES]
        mixed = []
        for half in (low, jnp.logical_not(low)):
            scores = lax.dot_general(
                jnp.where(half, queries, 0.0).astype(BF16), keys, (((1,), (1,)), ((), ())),
                preferred_element_type=F32,
            )
            scores = jnp.where(same, scores, -jnp.inf)
            expon = jnp.exp(scores - jnp.max(scores, axis=-1, keepdims=True))
            weights = (expon * (1.0 / jnp.sum(expon, axis=-1, keepdims=True))).astype(BF16)
            mixed.append(jnp.dot(weights, values, preferred_element_type=F32))
        result = jnp.where(low, mixed[0], mixed[1])
        att_send[:, :, col:col + LANES] = result.reshape(CLIP, pix, LANES).astype(BF16)
        if lo + LANES == split:
            give_back(3, att_send_a, att_recv_a)
    give_back(4, att_send_b, att_recv_b)
    arrive(3, CLIP, att_recv_a)
    partial = joined[...] + jnp.dot(
        flat(att_recv_a[...]).astype(BF16), wout_ref[:split, :], preferred_element_type=F32
    )
    arrive(4, CLIP, att_recv_b)
    out_ref[...] = (
        partial + jnp.dot(
            flat(att_recv_b[...]).astype(BF16), wout_ref[split:, :], preferred_element_type=F32
        )
    ).astype(BF16)
    if fused_entry:
        leave(0, n, zero_recv)
    leave(1, CLIP, stat_recv)
    leave(2, CLIP, norm_recv)
    leave(3, CLIP, att_recv_a)
    leave(4, CLIP, att_recv_b)


def body(
    skip, control, zero_weight, gn_gain, gn_bias, conv_weight, ln_gain, qkv_weight, out_weight
):
    f_dev, rows, chans = skip.shape
    n = lax.axis_size("frames")
    frames, pix_dev, _ = control.shape
    assert f_dev == 1 and n % CLIP == 0 and rows % CLIP == 0
    fused_entry = pix_dev % 8 == 0
    if fused_entry:
        entry = control.reshape(frames * pix_dev, chans)
        entry_block = (n, pix_dev, chans)
    else:
        zero_out = jnp.dot(
            control.reshape(-1, chans), zero_weight, preferred_element_type=F32
        ).astype(BF16).reshape(control.shape)
        entry = lax.all_to_all(
            zero_out, "frames", split_axis=0, concat_axis=1, tiled=True
        ).reshape(rows, chans)
        entry_block = (8, 8, LANES)
    pix = rows // CLIP
    block = (CLIP, pix, chans)
    early = (chans // LANES + 1) // 2 * LANES
    hbm_spec = pl.BlockSpec(memory_space=pltpu.HBM)
    vmem_spec = pl.BlockSpec(memory_space=pltpu.VMEM)
    call = pl.pallas_call(
        functools.partial(kernel, n, fused_entry),
        out_shape=jax.ShapeDtypeStruct((rows, chans), BF16),
        in_specs=[hbm_spec] * 9,
        out_specs=vmem_spec,
        scratch_shapes=[
            pltpu.VMEM((rows, chans), BF16),
            pltpu.VMEM(entry.shape, BF16),
            pltpu.VMEM(zero_weight.shape, BF16),
            pltpu.VMEM((3, 3 * chans, chans), BF16),
            pltpu.VMEM(qkv_weight.shape, BF16),
            pltpu.VMEM(out_weight.shape, BF16),
            pltpu.VMEM((chans,), F32),
            pltpu.VMEM((chans,), F32),
            pltpu.VMEM((chans,), F32),
            pltpu.VMEM(entry_block, BF16),
            pltpu.VMEM(entry_block, BF16),
            pltpu.VMEM((rows, chans), F32),
            pltpu.VMEM((1, LANES), F32),
            pltpu.VMEM((CLIP, 1, LANES), F32),
            pltpu.VMEM((rows + 2 * W, 3 * chans), BF16),
            pltpu.VMEM(block, BF16),
            pltpu.VMEM(block, BF16),
            pltpu.VMEM(block[:2] + (early,), BF16),
            pltpu.VMEM(block[:2] + (chans - early,), BF16),
            pltpu.VMEM(block[:2] + (early,), BF16),
            pltpu.VMEM(block[:2] + (chans - early,), BF16),
            pltpu.SemaphoreType.DMA((9,)),
            pltpu.SemaphoreType.DMA((5,)),
            pltpu.SemaphoreType.DMA((5,)),
        ],
        compiler_params=pltpu.CompilerParams(
            collective_id=0, has_side_effects=True, vmem_limit_bytes=60 * 1024 * 1024
        ),
    )
    out = call(
        skip.reshape(rows, chans), entry, zero_weight, gn_gain, gn_bias,
        conv_weight.reshape(3, 3 * chans, chans), ln_gain, qkv_weight, out_weight,
    )
    return out.reshape(skip.shape)


def solution(mesh):
    frames = P(("groups", "frames"), None, None)
    return jax.shard_map(
        body, mesh=mesh,
        in_specs=(frames, P("groups", "frames", None), P(), P(), P(), P(), P(), P(), P()),
        out_specs=frames, check_vma=False,
    )
```

```python
import functools
import math

import jax
import jax.numpy as jnp
from jax import lax
from jax.experimental import pallas as pl
from jax.experimental.pallas import tpu as pltpu
from jax.sharding import PartitionSpec as P

HEADS = 10
HD = 64
GROUPS = 32
CLIP = 32
W = 32
LANES = 128
HALVES = 2
EPS = 1e-05
MESH = pl.DeviceIdType.MESH
F32 = jnp.float32
BF16 = jnp.bfloat16


def parts(row):
    top = row.astype(BF16).astype(F32)
    middle = (row - top).astype(BF16).astype(F32)
    return [top, middle, row - top - middle]


def pool(first, second, matrix):
    rows = parts(first) + parts(second)
    lead = lax.broadcasted_iota(jnp.int32, (16, first.shape[1]), 0)
    stack = jnp.zeros(lead.shape, F32)
    for i, row in enumerate(rows):
        stack = jnp.where(lead == i, row, stack)
    product = jnp.dot(stack.astype(BF16), matrix, preferred_element_type=F32)
    return (
        product[0:1] + product[1:2] + product[2:3],
        product[3:4] + product[4:5] + product[5:6],
    )


def kernel(
    n, fused_entry,
    skip_hbm, entry_hbm, zero_hbm, gain_hbm, bias_hbm, conv_hbm, ln_hbm, qkv_hbm, wout_hbm,
    out_ref,
    skip_ref, entry_ref, zero_ref, conv_ref, qkv_ref, wout_ref, gain_ref, bias_ref, ln_ref,
    zero_send, zero_recv, joined, stat_send, stat_recv, window, norm_send, norm_recv,
    att_send, att_recv, load_sem, send_sem, recv_sem,
):
    me = lax.axis_index("frames")
    rows, chans = skip_ref.shape
    base = me // CLIP * CLIP
    spot = lax.rem(me, CLIP)
    per = CLIP // HALVES
    own_block = lax.rem(spot, HALVES) * per + spot // HALVES

    loads = [
        pltpu.make_async_copy(src, dst, load_sem.at[i])
        for i, (src, dst) in enumerate([
            (entry_hbm, entry_ref), (zero_hbm, zero_ref), (skip_hbm, skip_ref),
            (conv_hbm, conv_ref), (qkv_hbm, qkv_ref), (wout_hbm, wout_ref),
            (gain_hbm, gain_ref), (bias_hbm, bias_ref), (ln_hbm, ln_ref),
        ])
    ]
    for load in loads[:3]:
        load.start()

    barrier = pltpu.get_barrier_semaphore()
    first, count, mine = (0, n, me) if fused_entry else (base, CLIP, spot)

    for step in range(1, count):
        pl.semaphore_signal(
            barrier, inc=1, device_id={"frames": first + lax.rem(mine + step, count)},
            device_id_type=MESH,
        )

    def exchange(phase, origin, total, place, pick, recv, slot):
        for step in range(1, total):
            other = lax.rem(place + step, total)
            pltpu.make_async_remote_copy(
                src_ref=pick(other), dst_ref=recv.at[slot],
                send_sem=send_sem.at[phase], recv_sem=recv_sem.at[phase],
                device_id={"frames": origin + other}, device_id_type=MESH,
            ).start()

    def arrive(phase, total, recv):
        part = recv.at[pl.ds(0, total - 1)]
        pltpu.make_async_copy(part, part, recv_sem.at[phase]).wait()

    def leave(phase, total, recv):
        part = recv.at[pl.ds(0, total - 1)]
        pltpu.make_async_copy(part, part, send_sem.at[phase]).wait()

    def give_row(block, other):
        pltpu.make_async_remote_copy(
            src_ref=norm_send.at[block], dst_ref=norm_recv.at[spot],
            send_sem=send_sem.at[2], recv_sem=recv_sem.at[2],
            device_id={"frames": base + other}, device_id_type=MESH,
        ).start()

    def flat(value):
        return value.astype(F32).reshape(-1, value.shape[-1])

    loads[0].wait()
    loads[1].wait()
    for load in loads[3:]:
        load.start()
    if fused_entry:
        zero_out = jnp.dot(entry_ref[...], zero_ref[...], preferred_element_type=F32)
        zero_send[...] = zero_out.reshape(zero_send.shape).astype(BF16)
        zero_recv[me] = zero_send[me]
    pl.semaphore_wait(barrier, count - 1)
    if fused_entry:
        exchange(0, 0, n, me, lambda other: zero_send.at[other], zero_recv, me)

    width = chans // GROUPS
    members = (
        lax.broadcasted_iota(jnp.int32, (chans, LANES), 0) // width
        == lax.rem(lax.broadcasted_iota(jnp.int32, (chans, LANES), 1), GROUPS)
    ).astype(F32).astype(BF16)
    members_t = (
        lax.broadcasted_iota(jnp.int32, (LANES, chans), 1) // width
        == lax.rem(lax.broadcasted_iota(jnp.int32, (LANES, chans), 0), GROUPS)
    ).astype(F32).astype(BF16)
    window[:W, :] = jnp.zeros((W, window.shape[1]), BF16)
    window[rows + W:, :] = jnp.zeros((W, window.shape[1]), BF16)
    loads[2].wait()

    if fused_entry:
        arrive(0, n, zero_recv)
        entry = flat(zero_recv[...])
    else:
        entry = entry_ref[...].astype(F32)
    together = skip_ref[...].astype(F32) + entry
    joined[...] = together
    sums = jnp.sum(together, axis=0, keepdims=True)
    squares = jnp.sum(together * together, axis=0, keepdims=True)
    sums, squares = pool(sums, squares, members)
    lane = lax.broadcasted_iota(jnp.int32, (1, LANES), 1)
    stat_send[...] = jnp.where(lane < GROUPS, sums, squares)
    stat_recv[spot] = stat_send[...]
    exchange(1, base, CLIP, spot, lambda other: stat_send, stat_recv, spot)
    arrive(1, CLIP, stat_recv)
    size = float(CLIP * rows * width)
    totals = jnp.sum(stat_recv[...], axis=0) / size
    group_mean, group_sq = pool(
        jnp.where(lane < GROUPS, totals, 0.0),
        jnp.where((lane >= GROUPS) & (lane < 2 * GROUPS), totals, 0.0),
        members_t,
    )
    group_inv = lax.rsqrt(group_sq - group_mean * group_mean + EPS)
    loads[6].wait()
    loads[7].wait()
    gain = gain_ref[...].reshape(1, chans)
    bias = bias_ref[...].reshape(1, chans)
    value = (joined[...] - group_mean) * group_inv * gain + bias
    active = value / (1.0 + jnp.exp(-value))
    active = active.astype(BF16).astype(F32)

    column = lax.rem(lax.broadcasted_iota(jnp.int32, (rows, chans), 0), W)
    body_rows = slice(W, rows + W)
    window[body_rows, 0:chans] = jnp.where(column == 0, 0.0, pltpu.roll(active, 1, 0)).astype(BF16)
    window[body_rows, chans:2 * chans] = active.astype(BF16)
    window[body_rows, 2 * chans:] = jnp.where(
        column == W - 1, 0.0, pltpu.roll(active, rows - 1, 0)
    ).astype(BF16)
    loads[3].wait()
    loads[8].wait()
    ln_gain = ln_ref[...].reshape(1, chans)
    deep = rows // HALVES
    for half in range(HALVES):
        top = half * deep
        resid = joined[top:top + deep, :]
        for tap in range(3):
            start = top + tap * W
            resid = resid + jnp.dot(
                window[start:start + deep, :], conv_ref[tap], preferred_element_type=F32
            )
        joined[top:top + deep, :] = resid
        mean = jnp.mean(resid, axis=-1, keepdims=True)
        centred = resid - mean
        var = jnp.mean(centred * centred, axis=-1, keepdims=True)
        normed = centred * lax.rsqrt(var + EPS) * ln_gain
        norm_send[half * per:(half + 1) * per] = normed.reshape(
            (per,) + norm_send.shape[1:]
        ).astype(BF16)

        for step in range(1, per):
            place = lax.rem(spot // HALVES + step, per)
            give_row(half * per + place, place * HALVES + half)
    for step in range(1, HALVES):
        half = lax.rem(spot + step, HALVES)
        place = spot // HALVES
        give_row(half * per + place, place * HALVES + half)
    norm_recv[spot] = norm_send[own_block]
    loads[4].wait()
    loads[5].wait()
    arrive(2, CLIP, norm_recv)

    pix = norm_send.shape[1]
    tokens = flat(norm_recv[...]).astype(BF16)
    qkv = jnp.dot(tokens, qkv_ref[...], preferred_element_type=F32).astype(BF16)
    same = (
        lax.rem(lax.broadcasted_iota(jnp.int32, (rows, rows), 0), pix)
        == lax.rem(lax.broadcasted_iota(jnp.int32, (rows, rows), 1), pix)
    )
    low = lax.broadcasted_iota(jnp.int32, (rows, LANES), 1) < HD
    scale = 1.0 / math.sqrt(HD)
    for pair in range(chans // LANES):
        lo = pair * LANES
        queries = qkv[:, lo:lo + LANES].astype(F32) * scale
        keys = qkv[:, chans + lo:chans + lo + LANES]
        values = qkv[:, 2 * chans + lo:2 * chans + lo + LANES]
        mixed = []
        for half in (low, jnp.logical_not(low)):
            scores = lax.dot_general(
                jnp.where(half, queries, 0.0).astype(BF16), keys, (((1,), (1,)), ((), ())),
                preferred_element_type=F32,
            )
            scores = jnp.where(same, scores, -jnp.inf)
            expon = jnp.exp(scores - jnp.max(scores, axis=-1, keepdims=True))
            weights = (expon * (1.0 / jnp.sum(expon, axis=-1, keepdims=True))).astype(BF16)
            mixed.append(jnp.dot(weights, values, preferred_element_type=F32))
        result = jnp.where(low, mixed[0], mixed[1])
        att_send[:, :, lo:lo + LANES] = result.reshape(CLIP, pix, LANES).astype(BF16)
    att_recv[own_block] = att_send[spot]
    exchange(3, base, CLIP, spot, lambda other: att_send.at[other], att_recv, own_block)
    arrive(3, CLIP, att_recv)
    attended = flat(att_recv[...]).astype(BF16)
    out_ref[...] = (
        joined[...] + jnp.dot(attended, wout_ref[...], preferred_element_type=F32)
    ).astype(BF16)
    if fused_entry:
        leave(0, n, zero_recv)
    leave(1, CLIP, stat_recv)
    leave(2, CLIP, norm_recv)
    leave(3, CLIP, att_recv)


def body(
    skip, control, zero_weight, gn_gain, gn_bias, conv_weight, ln_gain, qkv_weight, out_weight
):
    f_dev, rows, chans = skip.shape
    n = lax.axis_size("frames")
    frames, pix_dev, _ = control.shape
    assert f_dev == 1 and n % CLIP == 0 and rows % CLIP == 0
    fused_entry = pix_dev % 8 == 0
    if fused_entry:
        entry = control.reshape(frames * pix_dev, chans)
        entry_block = (n, pix_dev, chans)
    else:
        zero_out = jnp.dot(
            control.reshape(-1, chans), zero_weight, preferred_element_type=F32
        ).astype(BF16).reshape(control.shape)
        entry = lax.all_to_all(
            zero_out, "frames", split_axis=0, concat_axis=1, tiled=True
        ).reshape(rows, chans)
        entry_block = (8, 8, LANES)
    pix = rows // CLIP
    block = (CLIP, pix, chans)
    hbm_spec = pl.BlockSpec(memory_space=pltpu.HBM)
    vmem_spec = pl.BlockSpec(memory_space=pltpu.VMEM)
    call = pl.pallas_call(
        functools.partial(kernel, n, fused_entry),
        out_shape=jax.ShapeDtypeStruct((rows, chans), BF16),
        in_specs=[hbm_spec] * 9,
        out_specs=vmem_spec,
        scratch_shapes=[
            pltpu.VMEM((rows, chans), BF16),
            pltpu.VMEM(entry.shape, BF16),
            pltpu.VMEM(zero_weight.shape, BF16),
            pltpu.VMEM((3, 3 * chans, chans), BF16),
            pltpu.VMEM(qkv_weight.shape, BF16),
            pltpu.VMEM(out_weight.shape, BF16),
            pltpu.VMEM((chans,), F32),
            pltpu.VMEM((chans,), F32),
            pltpu.VMEM((chans,), F32),
            pltpu.VMEM(entry_block, BF16),
            pltpu.VMEM(entry_block, BF16),
            pltpu.VMEM((rows, chans), F32),
            pltpu.VMEM((1, LANES), F32),
            pltpu.VMEM((CLIP, 1, LANES), F32),
            pltpu.VMEM((rows + 2 * W, 3 * chans), BF16),
            pltpu.VMEM(block, BF16),
            pltpu.VMEM(block, BF16),
            pltpu.VMEM(block, BF16),
            pltpu.VMEM(block, BF16),
            pltpu.SemaphoreType.DMA((9,)),
            pltpu.SemaphoreType.DMA((4,)),
            pltpu.SemaphoreType.DMA((4,)),
        ],
        compiler_params=pltpu.CompilerParams(
            collective_id=0, has_side_effects=True, vmem_limit_bytes=60 * 1024 * 1024
        ),
    )
    out = call(
        skip.reshape(rows, chans), entry, zero_weight, gn_gain, gn_bias,
        conv_weight.reshape(3, 3 * chans, chans), ln_gain, qkv_weight, out_weight,
    )
    return out.reshape(skip.shape)


def solution(mesh):
    frames = P(("groups", "frames"), None, None)
    return jax.shard_map(
        body, mesh=mesh,
        in_specs=(frames, P("groups", "frames", None), P(), P(), P(), P(), P(), P(), P()),
        out_specs=frames, check_vma=False,
    )
```

```python
import functools
import math

import jax
import jax.numpy as jnp
from jax import lax
from jax.experimental import pallas as pl
from jax.experimental.pallas import tpu as pltpu
from jax.sharding import PartitionSpec as P

HEADS = 10
HD = 64
GROUPS = 32
CLIP = 32
W = 32
LANES = 128
HALVES = 2
PIXEL_SETS = 2
EPS = 1e-05
MESH = pl.DeviceIdType.MESH
F32 = jnp.float32
BF16 = jnp.bfloat16


def parts(row):
    top = row.astype(BF16).astype(F32)
    middle = (row - top).astype(BF16).astype(F32)
    return [top, middle, row - top - middle]


def pool(first, second, matrix):
    rows = parts(first) + parts(second)
    lead = lax.broadcasted_iota(jnp.int32, (16, first.shape[1]), 0)
    stack = jnp.zeros(lead.shape, F32)
    for i, row in enumerate(rows):
        stack = jnp.where(lead == i, row, stack)
    product = jnp.dot(stack.astype(BF16), matrix, preferred_element_type=F32)
    return (
        product[0:1] + product[1:2] + product[2:3],
        product[3:4] + product[4:5] + product[5:6],
    )


def kernel(
    n, fused_entry,
    skip_hbm, entry_hbm, zero_hbm, gain_hbm, bias_hbm, conv_hbm, ln_hbm, qkv_hbm, wout_hbm,
    out_ref,
    skip_ref, entry_ref, zero_ref, conv_ref, qkv_ref, wout_ref, gain_ref, bias_ref, ln_ref,
    zero_send, zero_recv, joined, stat_send, stat_recv, window, norm_send, norm_recv,
    att_send, att_recv, att_sorted, load_sem, send_sem, recv_sem,
):
    me = lax.axis_index("frames")
    rows, chans = skip_ref.shape
    base = me // CLIP * CLIP
    spot = lax.rem(me, CLIP)
    per = CLIP // HALVES
    own_block = lax.rem(spot, HALVES) * per + spot // HALVES

    loads = [
        pltpu.make_async_copy(src, dst, load_sem.at[i])
        for i, (src, dst) in enumerate([
            (entry_hbm, entry_ref), (zero_hbm, zero_ref), (skip_hbm, skip_ref),
            (conv_hbm, conv_ref), (qkv_hbm, qkv_ref), (wout_hbm, wout_ref),
            (gain_hbm, gain_ref), (bias_hbm, bias_ref), (ln_hbm, ln_ref),
        ])
    ]
    for load in loads[:3]:
        load.start()

    barrier = pltpu.get_barrier_semaphore()
    first, count, mine = (0, n, me) if fused_entry else (base, CLIP, spot)

    for step in range(1, count):
        pl.semaphore_signal(
            barrier, inc=1, device_id={"frames": first + lax.rem(mine + step, count)},
            device_id_type=MESH,
        )

    def exchange(phase, origin, total, place, pick, recv, slot):
        for step in range(1, total):
            other = lax.rem(place + step, total)
            pltpu.make_async_remote_copy(
                src_ref=pick(other), dst_ref=recv.at[slot],
                send_sem=send_sem.at[phase], recv_sem=recv_sem.at[phase],
                device_id={"frames": origin + other}, device_id_type=MESH,
            ).start()

    def arrive(phase, total, recv):
        part = recv.at[pl.ds(0, total - 1)]
        pltpu.make_async_copy(part, part, recv_sem.at[phase]).wait()

    def leave(phase, total, recv):
        part = recv.at[pl.ds(0, total - 1)]
        pltpu.make_async_copy(part, part, send_sem.at[phase]).wait()

    def give_row(block, other):
        pltpu.make_async_remote_copy(
            src_ref=norm_send.at[block], dst_ref=norm_recv.at[spot],
            send_sem=send_sem.at[2], recv_sem=recv_sem.at[2],
            device_id={"frames": base + other}, device_id_type=MESH,
        ).start()

    def flat(value):
        return value.astype(F32).reshape(-1, value.shape[-1])

    loads[0].wait()
    loads[1].wait()
    for load in loads[3:]:
        load.start()
    if fused_entry:
        zero_out = jnp.dot(entry_ref[...], zero_ref[...], preferred_element_type=F32)
        zero_send[...] = zero_out.reshape(zero_send.shape).astype(BF16)
        zero_recv[me] = zero_send[me]
    pl.semaphore_wait(barrier, count - 1)
    if fused_entry:
        exchange(0, 0, n, me, lambda other: zero_send.at[other], zero_recv, me)

    width = chans // GROUPS
    members = (
        lax.broadcasted_iota(jnp.int32, (chans, LANES), 0) // width
        == lax.rem(lax.broadcasted_iota(jnp.int32, (chans, LANES), 1), GROUPS)
    ).astype(F32).astype(BF16)
    members_t = (
        lax.broadcasted_iota(jnp.int32, (LANES, chans), 1) // width
        == lax.rem(lax.broadcasted_iota(jnp.int32, (LANES, chans), 0), GROUPS)
    ).astype(F32).astype(BF16)
    window[:W, :] = jnp.zeros((W, window.shape[1]), BF16)
    window[rows + W:, :] = jnp.zeros((W, window.shape[1]), BF16)
    loads[2].wait()

    if fused_entry:
        arrive(0, n, zero_recv)
        entry = flat(zero_recv[...])
    else:
        entry = entry_ref[...].astype(F32)
    together = skip_ref[...].astype(F32) + entry
    joined[...] = together
    sums = jnp.sum(together, axis=0, keepdims=True)
    squares = jnp.sum(together * together, axis=0, keepdims=True)
    sums, squares = pool(sums, squares, members)
    lane = lax.broadcasted_iota(jnp.int32, (1, LANES), 1)
    stat_send[...] = jnp.where(lane < GROUPS, sums, squares)
    stat_recv[spot] = stat_send[...]
    exchange(1, base, CLIP, spot, lambda other: stat_send, stat_recv, spot)
    arrive(1, CLIP, stat_recv)
    size = float(CLIP * rows * width)
    totals = jnp.sum(stat_recv[...], axis=0) / size
    group_mean, group_sq = pool(
        jnp.where(lane < GROUPS, totals, 0.0),
        jnp.where((lane >= GROUPS) & (lane < 2 * GROUPS), totals, 0.0),
        members_t,
    )
    group_inv = lax.rsqrt(group_sq - group_mean * group_mean + EPS)
    loads[6].wait()
    loads[7].wait()
    gain = gain_ref[...].reshape(1, chans)
    bias = bias_ref[...].reshape(1, chans)
    value = (joined[...] - group_mean) * group_inv * gain + bias
    active = value / (1.0 + jnp.exp(-value))
    active = active.astype(BF16).astype(F32)

    column = lax.rem(lax.broadcasted_iota(jnp.int32, (rows, chans), 0), W)
    body_rows = slice(W, rows + W)
    window[body_rows, 0:chans] = jnp.where(column == 0, 0.0, pltpu.roll(active, 1, 0)).astype(BF16)
    window[body_rows, chans:2 * chans] = active.astype(BF16)
    window[body_rows, 2 * chans:] = jnp.where(
        column == W - 1, 0.0, pltpu.roll(active, rows - 1, 0)
    ).astype(BF16)
    loads[3].wait()
    loads[8].wait()
    ln_gain = ln_ref[...].reshape(1, chans)
    deep = rows // HALVES
    for half in range(HALVES):
        top = half * deep
        resid = joined[top:top + deep, :]
        for tap in range(3):
            start = top + tap * W
            resid = resid + jnp.dot(
                window[start:start + deep, :], conv_ref[tap], preferred_element_type=F32
            )
        joined[top:top + deep, :] = resid
        mean = jnp.mean(resid, axis=-1, keepdims=True)
        centred = resid - mean
        var = jnp.mean(centred * centred, axis=-1, keepdims=True)
        normed = centred * lax.rsqrt(var + EPS) * ln_gain
        norm_send[half * per:(half + 1) * per] = normed.reshape(
            (per,) + norm_send.shape[1:]
        ).astype(BF16)

        for step in range(1, per):
            place = lax.rem(spot // HALVES + step, per)
            give_row(half * per + place, place * HALVES + half)
    for step in range(1, HALVES):
        half = lax.rem(spot + step, HALVES)
        place = spot // HALVES
        give_row(half * per + place, place * HALVES + half)
    norm_recv[spot] = norm_send[own_block]
    pix = norm_send.shape[1]
    few = pix // PIXEL_SETS
    block = CLIP * few

    def source(sorted_row):
        within = lax.rem(sorted_row, block)
        return within // few * pix + sorted_row // block * few + lax.rem(within, few)

    across = lax.broadcasted_iota(jnp.int32, (rows, rows), 0)
    along = lax.broadcasted_iota(jnp.int32, (rows, rows), 1)
    order = (source(across) == along).astype(F32).astype(BF16)
    order_back = (source(along) == across).astype(F32).astype(BF16)
    loads[4].wait()
    loads[5].wait()
    arrive(2, CLIP, norm_recv)

    tokens = jnp.dot(
        order, flat(norm_recv[...]).astype(BF16), preferred_element_type=F32
    ).astype(BF16)
    qkv = jnp.dot(tokens, qkv_ref[...], preferred_element_type=F32).astype(BF16)
    same = (
        lax.rem(lax.broadcasted_iota(jnp.int32, (block, block), 0), few)
        == lax.rem(lax.broadcasted_iota(jnp.int32, (block, block), 1), few)
    )
    low = lax.broadcasted_iota(jnp.int32, (block, LANES), 1) < HD
    scale = 1.0 / math.sqrt(HD)
    for pair in range(chans // LANES):
        lo = pair * LANES
        for top in range(0, rows, block):
            queries = qkv[top:top + block, lo:lo + LANES].astype(F32) * scale
            keys = qkv[top:top + block, chans + lo:chans + lo + LANES]
            values = qkv[top:top + block, 2 * chans + lo:2 * chans + lo + LANES]
            mixed = []
            for half in (low, jnp.logical_not(low)):
                scores = lax.dot_general(
                    jnp.where(half, queries, 0.0).astype(BF16), keys, (((1,), (1,)), ((), ())),
                    preferred_element_type=F32,
                )
                scores = jnp.where(same, scores, -jnp.inf)
                expon = jnp.exp(scores - jnp.max(scores, axis=-1, keepdims=True))
                weights = (expon * (1.0 / jnp.sum(expon, axis=-1, keepdims=True))).astype(BF16)
                mixed.append(jnp.dot(weights, values, preferred_element_type=F32))
            att_sorted[top:top + block, lo:lo + LANES] = jnp.where(
                low, mixed[0], mixed[1]
            ).astype(BF16)
    att_send[...] = jnp.dot(
        order_back, att_sorted[...], preferred_element_type=F32
    ).reshape(att_send.shape).astype(BF16)
    att_recv[own_block] = att_send[spot]
    exchange(3, base, CLIP, spot, lambda other: att_send.at[other], att_recv, own_block)
    arrive(3, CLIP, att_recv)
    attended = flat(att_recv[...]).astype(BF16)
    out_ref[...] = (
        joined[...] + jnp.dot(attended, wout_ref[...], preferred_element_type=F32)
    ).astype(BF16)
    if fused_entry:
        leave(0, n, zero_recv)
    leave(1, CLIP, stat_recv)
    leave(2, CLIP, norm_recv)
    leave(3, CLIP, att_recv)


def body(
    skip, control, zero_weight, gn_gain, gn_bias, conv_weight, ln_gain, qkv_weight, out_weight
):
    f_dev, rows, chans = skip.shape
    n = lax.axis_size("frames")
    frames, pix_dev, _ = control.shape
    assert f_dev == 1 and n % CLIP == 0 and rows % CLIP == 0
    fused_entry = pix_dev % 8 == 0
    if fused_entry:
        entry = control.reshape(frames * pix_dev, chans)
        entry_block = (n, pix_dev, chans)
    else:
        zero_out = jnp.dot(
            control.reshape(-1, chans), zero_weight, preferred_element_type=F32
        ).astype(BF16).reshape(control.shape)
        entry = lax.all_to_all(
            zero_out, "frames", split_axis=0, concat_axis=1, tiled=True
        ).reshape(rows, chans)
        entry_block = (8, 8, LANES)
    pix = rows // CLIP
    block = (CLIP, pix, chans)
    hbm_spec = pl.BlockSpec(memory_space=pltpu.HBM)
    vmem_spec = pl.BlockSpec(memory_space=pltpu.VMEM)
    call = pl.pallas_call(
        functools.partial(kernel, n, fused_entry),
        out_shape=jax.ShapeDtypeStruct((rows, chans), BF16),
        in_specs=[hbm_spec] * 9,
        out_specs=vmem_spec,
        scratch_shapes=[
            pltpu.VMEM((rows, chans), BF16),
            pltpu.VMEM(entry.shape, BF16),
            pltpu.VMEM(zero_weight.shape, BF16),
            pltpu.VMEM((3, 3 * chans, chans), BF16),
            pltpu.VMEM(qkv_weight.shape, BF16),
            pltpu.VMEM(out_weight.shape, BF16),
            pltpu.VMEM((chans,), F32),
            pltpu.VMEM((chans,), F32),
            pltpu.VMEM((chans,), F32),
            pltpu.VMEM(entry_block, BF16),
            pltpu.VMEM(entry_block, BF16),
            pltpu.VMEM((rows, chans), F32),
            pltpu.VMEM((1, LANES), F32),
            pltpu.VMEM((CLIP, 1, LANES), F32),
            pltpu.VMEM((rows + 2 * W, 3 * chans), BF16),
            pltpu.VMEM(block, BF16),
            pltpu.VMEM(block, BF16),
            pltpu.VMEM(block, BF16),
            pltpu.VMEM(block, BF16),
            pltpu.VMEM((rows, chans), BF16),
            pltpu.SemaphoreType.DMA((9,)),
            pltpu.SemaphoreType.DMA((4,)),
            pltpu.SemaphoreType.DMA((4,)),
        ],
        compiler_params=pltpu.CompilerParams(
            collective_id=0, has_side_effects=True, vmem_limit_bytes=60 * 1024 * 1024
        ),
    )
    out = call(
        skip.reshape(rows, chans), entry, zero_weight, gn_gain, gn_bias,
        conv_weight.reshape(3, 3 * chans, chans), ln_gain, qkv_weight, out_weight,
    )
    return out.reshape(skip.shape)


def solution(mesh):
    frames = P(("groups", "frames"), None, None)
    return jax.shard_map(
        body, mesh=mesh,
        in_specs=(frames, P("groups", "frames", None), P(), P(), P(), P(), P(), P(), P()),
        out_specs=frames, check_vma=False,
    )
```

```python
import functools
import math

import jax
import jax.numpy as jnp
from jax import lax
from jax.experimental import pallas as pl
from jax.experimental.pallas import tpu as pltpu
from jax.sharding import PartitionSpec as P

HEADS = 10
HD = 64
GROUPS = 32
CLIP = 32
W = 32
LANES = 128
HALVES = 2
EPS = 1e-05
MESH = pl.DeviceIdType.MESH
F32 = jnp.float32
BF16 = jnp.bfloat16


def parts(row):
    top = row.astype(BF16).astype(F32)
    middle = (row - top).astype(BF16).astype(F32)
    return [top, middle, row - top - middle]


def pool(first, second, matrix):
    rows = parts(first) + parts(second)
    lead = lax.broadcasted_iota(jnp.int32, (16, first.shape[1]), 0)
    stack = jnp.zeros(lead.shape, F32)
    for i, row in enumerate(rows):
        stack = jnp.where(lead == i, row, stack)
    product = jnp.dot(stack.astype(BF16), matrix, preferred_element_type=F32)
    return (
        product[0:1] + product[1:2] + product[2:3],
        product[3:4] + product[4:5] + product[5:6],
    )


def kernel(
    n, fused_entry,
    skip_hbm, entry_hbm, zero_hbm, gain_hbm, bias_hbm, conv_hbm, ln_hbm, qkv_hbm, wout_hbm,
    out_ref,
    skip_ref, entry_ref, zero_ref, conv_ref, qkv_ref, wout_ref, gain_ref, bias_ref, ln_ref,
    zero_send, zero_recv, joined, stat_send, stat_recv, window, norm_send, norm_recv,
    att_send, att_recv, scores, weights, load_sem, send_sem, recv_sem,
):
    me = lax.axis_index("frames")
    rows, chans = skip_ref.shape
    base = me // CLIP * CLIP
    spot = lax.rem(me, CLIP)
    per = CLIP // HALVES
    own_block = lax.rem(spot, HALVES) * per + spot // HALVES

    loads = [
        pltpu.make_async_copy(src, dst, load_sem.at[i])
        for i, (src, dst) in enumerate([
            (entry_hbm, entry_ref), (zero_hbm, zero_ref), (skip_hbm, skip_ref),
            (conv_hbm, conv_ref), (qkv_hbm, qkv_ref), (wout_hbm, wout_ref),
            (gain_hbm, gain_ref), (bias_hbm, bias_ref), (ln_hbm, ln_ref),
        ])
    ]
    for load in loads[:3]:
        load.start()

    barrier = pltpu.get_barrier_semaphore()
    first, count, mine = (0, n, me) if fused_entry else (base, CLIP, spot)

    for step in range(1, count):
        pl.semaphore_signal(
            barrier, inc=1, device_id={"frames": first + lax.rem(mine + step, count)},
            device_id_type=MESH,
        )

    def exchange(phase, origin, total, place, pick, recv, slot):
        for step in range(1, total):
            other = lax.rem(place + step, total)
            pltpu.make_async_remote_copy(
                src_ref=pick(other), dst_ref=recv.at[slot],
                send_sem=send_sem.at[phase], recv_sem=recv_sem.at[phase],
                device_id={"frames": origin + other}, device_id_type=MESH,
            ).start()

    def arrive(phase, total, recv):
        part = recv.at[pl.ds(0, total - 1)]
        pltpu.make_async_copy(part, part, recv_sem.at[phase]).wait()

    def leave(phase, total, recv):
        part = recv.at[pl.ds(0, total - 1)]
        pltpu.make_async_copy(part, part, send_sem.at[phase]).wait()

    def give_row(block, other):
        pltpu.make_async_remote_copy(
            src_ref=norm_send.at[block], dst_ref=norm_recv.at[spot],
            send_sem=send_sem.at[2], recv_sem=recv_sem.at[2],
            device_id={"frames": base + other}, device_id_type=MESH,
        ).start()

    def flat(value):
        return value.astype(F32).reshape(-1, value.shape[-1])

    loads[0].wait()
    loads[1].wait()
    for load in loads[3:]:
        load.start()
    if fused_entry:
        zero_out = jnp.dot(entry_ref[...], zero_ref[...], preferred_element_type=F32)
        zero_send[...] = zero_out.reshape(zero_send.shape).astype(BF16)
        zero_recv[me] = zero_send[me]
    pl.semaphore_wait(barrier, count - 1)
    if fused_entry:
        exchange(0, 0, n, me, lambda other: zero_send.at[other], zero_recv, me)

    width = chans // GROUPS
    members = (
        lax.broadcasted_iota(jnp.int32, (chans, LANES), 0) // width
        == lax.rem(lax.broadcasted_iota(jnp.int32, (chans, LANES), 1), GROUPS)
    ).astype(F32).astype(BF16)
    members_t = (
        lax.broadcasted_iota(jnp.int32, (LANES, chans), 1) // width
        == lax.rem(lax.broadcasted_iota(jnp.int32, (LANES, chans), 0), GROUPS)
    ).astype(F32).astype(BF16)
    window[:W, :] = jnp.zeros((W, window.shape[1]), BF16)
    window[rows + W:, :] = jnp.zeros((W, window.shape[1]), BF16)
    loads[2].wait()

    if fused_entry:
        arrive(0, n, zero_recv)
        entry = flat(zero_recv[...])
    else:
        entry = entry_ref[...].astype(F32)
    together = skip_ref[...].astype(F32) + entry
    joined[...] = together
    sums = jnp.sum(together, axis=0, keepdims=True)
    squares = jnp.sum(together * together, axis=0, keepdims=True)
    sums, squares = pool(sums, squares, members)
    lane = lax.broadcasted_iota(jnp.int32, (1, LANES), 1)
    stat_send[...] = jnp.where(lane < GROUPS, sums, squares)
    stat_recv[spot] = stat_send[...]
    exchange(1, base, CLIP, spot, lambda other: stat_send, stat_recv, spot)
    arrive(1, CLIP, stat_recv)
    size = float(CLIP * rows * width)
    totals = jnp.sum(stat_recv[...], axis=0) / size
    group_mean, group_sq = pool(
        jnp.where(lane < GROUPS, totals, 0.0),
        jnp.where((lane >= GROUPS) & (lane < 2 * GROUPS), totals, 0.0),
        members_t,
    )
    group_inv = lax.rsqrt(group_sq - group_mean * group_mean + EPS)
    loads[6].wait()
    loads[7].wait()
    gain = gain_ref[...].reshape(1, chans)
    bias = bias_ref[...].reshape(1, chans)
    value = (joined[...] - group_mean) * group_inv * gain + bias
    active = value / (1.0 + jnp.exp(-value))
    active = active.astype(BF16).astype(F32)

    column = lax.rem(lax.broadcasted_iota(jnp.int32, (rows, chans), 0), W)
    body_rows = slice(W, rows + W)
    window[body_rows, 0:chans] = jnp.where(column == 0, 0.0, pltpu.roll(active, 1, 0)).astype(BF16)
    window[body_rows, chans:2 * chans] = active.astype(BF16)
    window[body_rows, 2 * chans:] = jnp.where(
        column == W - 1, 0.0, pltpu.roll(active, rows - 1, 0)
    ).astype(BF16)
    loads[3].wait()
    loads[8].wait()
    ln_gain = ln_ref[...].reshape(1, chans)
    deep = rows // HALVES
    for half in range(HALVES):
        top = half * deep
        resid = joined[top:top + deep, :]
        for tap in range(3):
            start = top + tap * W
            resid = resid + jnp.dot(
                window[start:start + deep, :], conv_ref[tap], preferred_element_type=F32
            )
        joined[top:top + deep, :] = resid
        mean = jnp.mean(resid, axis=-1, keepdims=True)
        centred = resid - mean
        var = jnp.mean(centred * centred, axis=-1, keepdims=True)
        normed = centred * lax.rsqrt(var + EPS) * ln_gain
        norm_send[half * per:(half + 1) * per] = normed.reshape(
            (per,) + norm_send.shape[1:]
        ).astype(BF16)

        for step in range(1, per):
            place = lax.rem(spot // HALVES + step, per)
            give_row(half * per + place, place * HALVES + half)
    for step in range(1, HALVES):
        half = lax.rem(spot + step, HALVES)
        place = spot // HALVES
        give_row(half * per + place, place * HALVES + half)
    norm_recv[spot] = norm_send[own_block]
    loads[4].wait()
    loads[5].wait()
    arrive(2, CLIP, norm_recv)

    pix = norm_send.shape[1]
    tokens = flat(norm_recv[...]).astype(BF16)
    qkv = jnp.dot(tokens, qkv_ref[...], preferred_element_type=F32).astype(BF16)
    same = (
        lax.rem(lax.broadcasted_iota(jnp.int32, (rows, rows), 0), pix)
        == lax.rem(lax.broadcasted_iota(jnp.int32, (rows, rows), 1), pix)
    )
    low = lax.broadcasted_iota(jnp.int32, (rows, LANES), 1) < HD
    scale = 1.0 / math.sqrt(HD)
    halves = (low, jnp.logical_not(low))
    pairs = chans // LANES
    for pair in range(pairs):
        lo = pair * LANES
        queries = qkv[:, lo:lo + LANES].astype(F32) * scale
        keys = qkv[:, chans + lo:chans + lo + LANES]
        for side, half in enumerate(halves):
            scores[2 * pair + side] = lax.dot_general(
                jnp.where(half, queries, 0.0).astype(BF16), keys, (((1,), (1,)), ((), ())),
                preferred_element_type=F32,
            )
    for head in range(2 * pairs):
        masked = jnp.where(same, scores[head], -jnp.inf)
        expon = jnp.exp(masked - jnp.max(masked, axis=-1, keepdims=True))
        weights[head] = (expon * (1.0 / jnp.sum(expon, axis=-1, keepdims=True))).astype(BF16)
    for pair in range(pairs):
        lo = pair * LANES
        values = qkv[:, 2 * chans + lo:2 * chans + lo + LANES]
        mixed = [
            jnp.dot(weights[2 * pair + side], values, preferred_element_type=F32)
            for side in range(2)
        ]
        result = jnp.where(low, mixed[0], mixed[1])
        att_send[:, :, lo:lo + LANES] = result.reshape(CLIP, pix, LANES).astype(BF16)
    att_recv[own_block] = att_send[spot]
    exchange(3, base, CLIP, spot, lambda other: att_send.at[other], att_recv, own_block)
    arrive(3, CLIP, att_recv)
    attended = flat(att_recv[...]).astype(BF16)
    out_ref[...] = (
        joined[...] + jnp.dot(attended, wout_ref[...], preferred_element_type=F32)
    ).astype(BF16)
    if fused_entry:
        leave(0, n, zero_recv)
    leave(1, CLIP, stat_recv)
    leave(2, CLIP, norm_recv)
    leave(3, CLIP, att_recv)


def body(
    skip, control, zero_weight, gn_gain, gn_bias, conv_weight, ln_gain, qkv_weight, out_weight
):
    f_dev, rows, chans = skip.shape
    n = lax.axis_size("frames")
    frames, pix_dev, _ = control.shape
    assert f_dev == 1 and n % CLIP == 0 and rows % CLIP == 0
    fused_entry = pix_dev % 8 == 0
    if fused_entry:
        entry = control.reshape(frames * pix_dev, chans)
        entry_block = (n, pix_dev, chans)
    else:
        zero_out = jnp.dot(
            control.reshape(-1, chans), zero_weight, preferred_element_type=F32
        ).astype(BF16).reshape(control.shape)
        entry = lax.all_to_all(
            zero_out, "frames", split_axis=0, concat_axis=1, tiled=True
        ).reshape(rows, chans)
        entry_block = (8, 8, LANES)
    pix = rows // CLIP
    block = (CLIP, pix, chans)
    hbm_spec = pl.BlockSpec(memory_space=pltpu.HBM)
    vmem_spec = pl.BlockSpec(memory_space=pltpu.VMEM)
    call = pl.pallas_call(
        functools.partial(kernel, n, fused_entry),
        out_shape=jax.ShapeDtypeStruct((rows, chans), BF16),
        in_specs=[hbm_spec] * 9,
        out_specs=vmem_spec,
        scratch_shapes=[
            pltpu.VMEM((rows, chans), BF16),
            pltpu.VMEM(entry.shape, BF16),
            pltpu.VMEM(zero_weight.shape, BF16),
            pltpu.VMEM((3, 3 * chans, chans), BF16),
            pltpu.VMEM(qkv_weight.shape, BF16),
            pltpu.VMEM(out_weight.shape, BF16),
            pltpu.VMEM((chans,), F32),
            pltpu.VMEM((chans,), F32),
            pltpu.VMEM((chans,), F32),
            pltpu.VMEM(entry_block, BF16),
            pltpu.VMEM(entry_block, BF16),
            pltpu.VMEM((rows, chans), F32),
            pltpu.VMEM((1, LANES), F32),
            pltpu.VMEM((CLIP, 1, LANES), F32),
            pltpu.VMEM((rows + 2 * W, 3 * chans), BF16),
            pltpu.VMEM(block, BF16),
            pltpu.VMEM(block, BF16),
            pltpu.VMEM(block, BF16),
            pltpu.VMEM(block, BF16),
            pltpu.VMEM((HEADS, rows, rows), F32),
            pltpu.VMEM((HEADS, rows, rows), BF16),
            pltpu.SemaphoreType.DMA((9,)),
            pltpu.SemaphoreType.DMA((4,)),
            pltpu.SemaphoreType.DMA((4,)),
        ],
        compiler_params=pltpu.CompilerParams(
            collective_id=0, has_side_effects=True, vmem_limit_bytes=60 * 1024 * 1024
        ),
    )
    out = call(
        skip.reshape(rows, chans), entry, zero_weight, gn_gain, gn_bias,
        conv_weight.reshape(3, 3 * chans, chans), ln_gain, qkv_weight, out_weight,
    )
    return out.reshape(skip.shape)


def solution(mesh):
    frames = P(("groups", "frames"), None, None)
    return jax.shard_map(
        body, mesh=mesh,
        in_specs=(frames, P("groups", "frames", None), P(), P(), P(), P(), P(), P(), P()),
        out_specs=frames, check_vma=False,
    )
```

```python
import functools
import math

import jax
import jax.numpy as jnp
from jax import lax
from jax.experimental import pallas as pl
from jax.experimental.pallas import tpu as pltpu
from jax.sharding import PartitionSpec as P

HEADS = 10
HD = 64
GROUPS = 32
CLIP = 32
W = 32
LANES = 128
HALVES = 2
EPS = 1e-05
MESH = pl.DeviceIdType.MESH
F32 = jnp.float32
BF16 = jnp.bfloat16


def far_first(total):
    return [*range(total // 4, total), *range(1, total // 4)]


def parts(row):
    top = row.astype(BF16).astype(F32)
    middle = (row - top).astype(BF16).astype(F32)
    return [top, middle, row - top - middle]


def pool(first, second, matrix):
    rows = parts(first) + parts(second)
    lead = lax.broadcasted_iota(jnp.int32, (16, first.shape[1]), 0)
    stack = jnp.zeros(lead.shape, F32)
    for i, row in enumerate(rows):
        stack = jnp.where(lead == i, row, stack)
    product = jnp.dot(stack.astype(BF16), matrix, preferred_element_type=F32)
    return (
        product[0:1] + product[1:2] + product[2:3],
        product[3:4] + product[4:5] + product[5:6],
    )


def kernel(
    n, fused_entry,
    skip_hbm, entry_hbm, zero_hbm, gain_hbm, bias_hbm, conv_hbm, ln_hbm, qkv_hbm, wout_hbm,
    out_ref,
    skip_ref, entry_ref, zero_ref, conv_ref, qkv_ref, wout_ref, gain_ref, bias_ref, ln_ref,
    zero_send, zero_recv, joined, stat_send, stat_recv, window, norm_send, norm_recv,
    att_send, att_recv, scores, weights, load_sem, send_sem, recv_sem,
):
    me = lax.axis_index("frames")
    rows, chans = skip_ref.shape
    base = me // CLIP * CLIP
    spot = lax.rem(me, CLIP)
    per = CLIP // HALVES
    own_block = lax.rem(spot, HALVES) * per + spot // HALVES

    loads = [
        pltpu.make_async_copy(src, dst, load_sem.at[i])
        for i, (src, dst) in enumerate([
            (entry_hbm, entry_ref), (zero_hbm, zero_ref), (skip_hbm, skip_ref),
            (conv_hbm, conv_ref), (qkv_hbm, qkv_ref), (wout_hbm, wout_ref),
            (gain_hbm, gain_ref), (bias_hbm, bias_ref), (ln_hbm, ln_ref),
        ])
    ]
    for load in loads[:3]:
        load.start()

    barrier = pltpu.get_barrier_semaphore()
    first, count, mine = (0, n, me) if fused_entry else (base, CLIP, spot)

    for step in range(1, count):
        pl.semaphore_signal(
            barrier, inc=1, device_id={"frames": first + lax.rem(mine + step, count)},
            device_id_type=MESH,
        )

    def exchange(phase, origin, total, place, pick, recv, slot):
        for step in far_first(total):
            other = lax.rem(place + step, total)
            pltpu.make_async_remote_copy(
                src_ref=pick(other), dst_ref=recv.at[slot],
                send_sem=send_sem.at[phase], recv_sem=recv_sem.at[phase],
                device_id={"frames": origin + other}, device_id_type=MESH,
            ).start()

    def arrive(phase, total, recv):
        part = recv.at[pl.ds(0, total - 1)]
        pltpu.make_async_copy(part, part, recv_sem.at[phase]).wait()

    def leave(phase, total, recv):
        part = recv.at[pl.ds(0, total - 1)]
        pltpu.make_async_copy(part, part, send_sem.at[phase]).wait()

    def give_row(block, other):
        pltpu.make_async_remote_copy(
            src_ref=norm_send.at[block], dst_ref=norm_recv.at[spot],
            send_sem=send_sem.at[2], recv_sem=recv_sem.at[2],
            device_id={"frames": base + other}, device_id_type=MESH,
        ).start()

    def flat(value):
        return value.astype(F32).reshape(-1, value.shape[-1])

    loads[0].wait()
    loads[1].wait()
    for load in loads[3:]:
        load.start()
    if fused_entry:
        zero_out = jnp.dot(entry_ref[...], zero_ref[...], preferred_element_type=F32)
        zero_send[...] = zero_out.reshape(zero_send.shape).astype(BF16)
        zero_recv[me] = zero_send[me]
    pl.semaphore_wait(barrier, count - 1)
    if fused_entry:
        exchange(0, 0, n, me, lambda other: zero_send.at[other], zero_recv, me)

    width = chans // GROUPS
    members = (
        lax.broadcasted_iota(jnp.int32, (chans, LANES), 0) // width
        == lax.rem(lax.broadcasted_iota(jnp.int32, (chans, LANES), 1), GROUPS)
    ).astype(F32).astype(BF16)
    members_t = (
        lax.broadcasted_iota(jnp.int32, (LANES, chans), 1) // width
        == lax.rem(lax.broadcasted_iota(jnp.int32, (LANES, chans), 0), GROUPS)
    ).astype(F32).astype(BF16)
    window[:W, :] = jnp.zeros((W, window.shape[1]), BF16)
    window[rows + W:, :] = jnp.zeros((W, window.shape[1]), BF16)
    loads[2].wait()

    if fused_entry:
        arrive(0, n, zero_recv)
        entry = flat(zero_recv[...])
    else:
        entry = entry_ref[...].astype(F32)
    together = skip_ref[...].astype(F32) + entry
    joined[...] = together
    sums = jnp.sum(together, axis=0, keepdims=True)
    squares = jnp.sum(together * together, axis=0, keepdims=True)
    sums, squares = pool(sums, squares, members)
    lane = lax.broadcasted_iota(jnp.int32, (1, LANES), 1)
    stat_send[...] = jnp.where(lane < GROUPS, sums, squares)
    stat_recv[spot] = stat_send[...]
    exchange(1, base, CLIP, spot, lambda other: stat_send, stat_recv, spot)
    arrive(1, CLIP, stat_recv)
    size = float(CLIP * rows * width)
    totals = jnp.sum(stat_recv[...], axis=0) / size
    group_mean, group_sq = pool(
        jnp.where(lane < GROUPS, totals, 0.0),
        jnp.where((lane >= GROUPS) & (lane < 2 * GROUPS), totals, 0.0),
        members_t,
    )
    group_inv = lax.rsqrt(group_sq - group_mean * group_mean + EPS)
    loads[6].wait()
    loads[7].wait()
    gain = gain_ref[...].reshape(1, chans)
    bias = bias_ref[...].reshape(1, chans)
    value = (joined[...] - group_mean) * group_inv * gain + bias
    active = value / (1.0 + jnp.exp(-value))
    active = active.astype(BF16).astype(F32)

    column = lax.rem(lax.broadcasted_iota(jnp.int32, (rows, chans), 0), W)
    body_rows = slice(W, rows + W)
    window[body_rows, 0:chans] = jnp.where(column == 0, 0.0, pltpu.roll(active, 1, 0)).astype(BF16)
    window[body_rows, chans:2 * chans] = active.astype(BF16)
    window[body_rows, 2 * chans:] = jnp.where(
        column == W - 1, 0.0, pltpu.roll(active, rows - 1, 0)
    ).astype(BF16)
    loads[3].wait()
    loads[8].wait()
    ln_gain = ln_ref[...].reshape(1, chans)
    deep = rows // HALVES
    for half in range(HALVES):
        top = half * deep
        resid = joined[top:top + deep, :]
        for tap in range(3):
            start = top + tap * W
            resid = resid + jnp.dot(
                window[start:start + deep, :], conv_ref[tap], preferred_element_type=F32
            )
        joined[top:top + deep, :] = resid
        mean = jnp.mean(resid, axis=-1, keepdims=True)
        centred = resid - mean
        var = jnp.mean(centred * centred, axis=-1, keepdims=True)
        normed = centred * lax.rsqrt(var + EPS) * ln_gain
        norm_send[half * per:(half + 1) * per] = normed.reshape(
            (per,) + norm_send.shape[1:]
        ).astype(BF16)

        for step in far_first(per):
            place = lax.rem(spot // HALVES + step, per)
            give_row(half * per + place, place * HALVES + half)
    for step in range(1, HALVES):
        half = lax.rem(spot + step, HALVES)
        place = spot // HALVES
        give_row(half * per + place, place * HALVES + half)
    norm_recv[spot] = norm_send[own_block]
    loads[4].wait()
    loads[5].wait()
    arrive(2, CLIP, norm_recv)

    pix = norm_send.shape[1]
    tokens = flat(norm_recv[...]).astype(BF16)
    qkv = jnp.dot(tokens, qkv_ref[...], preferred_element_type=F32).astype(BF16)
    same = (
        lax.rem(lax.broadcasted_iota(jnp.int32, (rows, rows), 0), pix)
        == lax.rem(lax.broadcasted_iota(jnp.int32, (rows, rows), 1), pix)
    )
    low = lax.broadcasted_iota(jnp.int32, (rows, LANES), 1) < HD
    scale = 1.0 / math.sqrt(HD)
    halves = (low, jnp.logical_not(low))
    pairs = chans // LANES
    for pair in range(pairs):
        lo = pair * LANES
        queries = qkv[:, lo:lo + LANES].astype(F32) * scale
        keys = qkv[:, chans + lo:chans + lo + LANES]
        for side, half in enumerate(halves):
            scores[2 * pair + side] = lax.dot_general(
                jnp.where(half, queries, 0.0).astype(BF16), keys, (((1,), (1,)), ((), ())),
                preferred_element_type=F32,
            )
    for head in range(2 * pairs):
        masked = jnp.where(same, scores[head], -jnp.inf)
        expon = jnp.exp(masked - jnp.max(masked, axis=-1, keepdims=True))
        weights[head] = (expon * (1.0 / jnp.sum(expon, axis=-1, keepdims=True))).astype(BF16)
    for pair in range(pairs):
        lo = pair * LANES
        values = qkv[:, 2 * chans + lo:2 * chans + lo + LANES]
        mixed = [
            jnp.dot(weights[2 * pair + side], values, preferred_element_type=F32)
            for side in range(2)
        ]
        result = jnp.where(low, mixed[0], mixed[1])
        att_send[:, :, lo:lo + LANES] = result.reshape(CLIP, pix, LANES).astype(BF16)
    att_recv[own_block] = att_send[spot]
    exchange(3, base, CLIP, spot, lambda other: att_send.at[other], att_recv, own_block)
    arrive(3, CLIP, att_recv)
    attended = flat(att_recv[...]).astype(BF16)
    out_ref[...] = (
        joined[...] + jnp.dot(attended, wout_ref[...], preferred_element_type=F32)
    ).astype(BF16)
    if fused_entry:
        leave(0, n, zero_recv)
    leave(1, CLIP, stat_recv)
    leave(2, CLIP, norm_recv)
    leave(3, CLIP, att_recv)


def body(
    skip, control, zero_weight, gn_gain, gn_bias, conv_weight, ln_gain, qkv_weight, out_weight
):
    f_dev, rows, chans = skip.shape
    n = lax.axis_size("frames")
    frames, pix_dev, _ = control.shape
    assert f_dev == 1 and n % CLIP == 0 and rows % CLIP == 0
    fused_entry = pix_dev % 8 == 0
    if fused_entry:
        entry = control.reshape(frames * pix_dev, chans)
        entry_block = (n, pix_dev, chans)
    else:
        zero_out = jnp.dot(
            control.reshape(-1, chans), zero_weight, preferred_element_type=F32
        ).astype(BF16).reshape(control.shape)
        entry = lax.all_to_all(
            zero_out, "frames", split_axis=0, concat_axis=1, tiled=True
        ).reshape(rows, chans)
        entry_block = (8, 8, LANES)
    pix = rows // CLIP
    block = (CLIP, pix, chans)
    hbm_spec = pl.BlockSpec(memory_space=pltpu.HBM)
    vmem_spec = pl.BlockSpec(memory_space=pltpu.VMEM)
    call = pl.pallas_call(
        functools.partial(kernel, n, fused_entry),
        out_shape=jax.ShapeDtypeStruct((rows, chans), BF16),
        in_specs=[hbm_spec] * 9,
        out_specs=vmem_spec,
        scratch_shapes=[
            pltpu.VMEM((rows, chans), BF16),
            pltpu.VMEM(entry.shape, BF16),
            pltpu.VMEM(zero_weight.shape, BF16),
            pltpu.VMEM((3, 3 * chans, chans), BF16),
            pltpu.VMEM(qkv_weight.shape, BF16),
            pltpu.VMEM(out_weight.shape, BF16),
            pltpu.VMEM((chans,), F32),
            pltpu.VMEM((chans,), F32),
            pltpu.VMEM((chans,), F32),
            pltpu.VMEM(entry_block, BF16),
            pltpu.VMEM(entry_block, BF16),
            pltpu.VMEM((rows, chans), F32),
            pltpu.VMEM((1, LANES), F32),
            pltpu.VMEM((CLIP, 1, LANES), F32),
            pltpu.VMEM((rows + 2 * W, 3 * chans), BF16),
            pltpu.VMEM(block, BF16),
            pltpu.VMEM(block, BF16),
            pltpu.VMEM(block, BF16),
            pltpu.VMEM(block, BF16),
            pltpu.VMEM((HEADS, rows, rows), F32),
            pltpu.VMEM((HEADS, rows, rows), BF16),
            pltpu.SemaphoreType.DMA((9,)),
            pltpu.SemaphoreType.DMA((4,)),
            pltpu.SemaphoreType.DMA((4,)),
        ],
        compiler_params=pltpu.CompilerParams(
            collective_id=0, has_side_effects=True, vmem_limit_bytes=60 * 1024 * 1024
        ),
    )
    out = call(
        skip.reshape(rows, chans), entry, zero_weight, gn_gain, gn_bias,
        conv_weight.reshape(3, 3 * chans, chans), ln_gain, qkv_weight, out_weight,
    )
    return out.reshape(skip.shape)


def solution(mesh):
    frames = P(("groups", "frames"), None, None)
    return jax.shard_map(
        body, mesh=mesh,
        in_specs=(frames, P("groups", "frames", None), P(), P(), P(), P(), P(), P(), P()),
        out_specs=frames, check_vma=False,
    )
```

```python
import functools
import math

import jax
import jax.numpy as jnp
from jax import lax
from jax.experimental import pallas as pl
from jax.experimental.pallas import tpu as pltpu
from jax.sharding import PartitionSpec as P

HEADS = 10
HD = 64
GROUPS = 32
CLIP = 32
W = 32
LANES = 128
HALVES = 2
EPS = 1e-05
MESH = pl.DeviceIdType.MESH
F32 = jnp.float32
BF16 = jnp.bfloat16


def both_ways(total):
    return sorted(range(1, total), key=lambda step: min(step, total - step))


def parts(row):
    top = row.astype(BF16).astype(F32)
    middle = (row - top).astype(BF16).astype(F32)
    return [top, middle, row - top - middle]


def pool(first, second, matrix):
    rows = parts(first) + parts(second)
    lead = lax.broadcasted_iota(jnp.int32, (16, first.shape[1]), 0)
    stack = jnp.zeros(lead.shape, F32)
    for i, row in enumerate(rows):
        stack = jnp.where(lead == i, row, stack)
    product = jnp.dot(stack.astype(BF16), matrix, preferred_element_type=F32)
    return (
        product[0:1] + product[1:2] + product[2:3],
        product[3:4] + product[4:5] + product[5:6],
    )


def kernel(
    n, fused_entry,
    skip_hbm, entry_hbm, zero_hbm, gain_hbm, bias_hbm, conv_hbm, ln_hbm, qkv_hbm, wout_hbm,
    out_ref,
    skip_ref, entry_ref, zero_ref, conv_ref, qkv_ref, wout_ref, gain_ref, bias_ref, ln_ref,
    zero_send, zero_recv, joined, stat_send, stat_recv, window, norm_send, norm_recv,
    att_send, att_recv, scores, weights, load_sem, send_sem, recv_sem,
):
    me = lax.axis_index("frames")
    rows, chans = skip_ref.shape
    base = me // CLIP * CLIP
    spot = lax.rem(me, CLIP)
    per = CLIP // HALVES
    own_block = lax.rem(spot, HALVES) * per + spot // HALVES

    loads = [
        pltpu.make_async_copy(src, dst, load_sem.at[i])
        for i, (src, dst) in enumerate([
            (entry_hbm, entry_ref), (zero_hbm, zero_ref), (skip_hbm, skip_ref),
            (conv_hbm, conv_ref), (qkv_hbm, qkv_ref), (wout_hbm, wout_ref),
            (gain_hbm, gain_ref), (bias_hbm, bias_ref), (ln_hbm, ln_ref),
        ])
    ]
    for load in loads[:3]:
        load.start()

    barrier = pltpu.get_barrier_semaphore()
    first, count, mine = (0, n, me) if fused_entry else (base, CLIP, spot)

    for step in range(1, count):
        pl.semaphore_signal(
            barrier, inc=1, device_id={"frames": first + lax.rem(mine + step, count)},
            device_id_type=MESH,
        )

    def exchange(phase, origin, total, place, pick, recv, slot):
        for step in both_ways(total):
            other = lax.rem(place + step, total)
            pltpu.make_async_remote_copy(
                src_ref=pick(other), dst_ref=recv.at[slot],
                send_sem=send_sem.at[phase], recv_sem=recv_sem.at[phase],
                device_id={"frames": origin + other}, device_id_type=MESH,
            ).start()

    def arrive(phase, total, recv):
        part = recv.at[pl.ds(0, total - 1)]
        pltpu.make_async_copy(part, part, recv_sem.at[phase]).wait()

    def leave(phase, total, recv):
        part = recv.at[pl.ds(0, total - 1)]
        pltpu.make_async_copy(part, part, send_sem.at[phase]).wait()

    def give_row(block, other):
        pltpu.make_async_remote_copy(
            src_ref=norm_send.at[block], dst_ref=norm_recv.at[spot],
            send_sem=send_sem.at[2], recv_sem=recv_sem.at[2],
            device_id={"frames": base + other}, device_id_type=MESH,
        ).start()

    def flat(value):
        return value.astype(F32).reshape(-1, value.shape[-1])

    loads[0].wait()
    loads[1].wait()
    for load in loads[3:]:
        load.start()
    if fused_entry:
        zero_out = jnp.dot(entry_ref[...], zero_ref[...], preferred_element_type=F32)
        zero_send[...] = zero_out.reshape(zero_send.shape).astype(BF16)
        zero_recv[me] = zero_send[me]
    pl.semaphore_wait(barrier, count - 1)
    if fused_entry:
        exchange(0, 0, n, me, lambda other: zero_send.at[other], zero_recv, me)

    width = chans // GROUPS
    members = (
        lax.broadcasted_iota(jnp.int32, (chans, LANES), 0) // width
        == lax.rem(lax.broadcasted_iota(jnp.int32, (chans, LANES), 1), GROUPS)
    ).astype(F32).astype(BF16)
    members_t = (
        lax.broadcasted_iota(jnp.int32, (LANES, chans), 1) // width
        == lax.rem(lax.broadcasted_iota(jnp.int32, (LANES, chans), 0), GROUPS)
    ).astype(F32).astype(BF16)
    window[:W, :] = jnp.zeros((W, window.shape[1]), BF16)
    window[rows + W:, :] = jnp.zeros((W, window.shape[1]), BF16)
    loads[2].wait()

    if fused_entry:
        arrive(0, n, zero_recv)
        entry = flat(zero_recv[...])
    else:
        entry = entry_ref[...].astype(F32)
    together = skip_ref[...].astype(F32) + entry
    joined[...] = together
    sums = jnp.sum(together, axis=0, keepdims=True)
    squares = jnp.sum(together * together, axis=0, keepdims=True)
    sums, squares = pool(sums, squares, members)
    lane = lax.broadcasted_iota(jnp.int32, (1, LANES), 1)
    stat_send[...] = jnp.where(lane < GROUPS, sums, squares)
    stat_recv[spot] = stat_send[...]
    exchange(1, base, CLIP, spot, lambda other: stat_send, stat_recv, spot)
    arrive(1, CLIP, stat_recv)
    size = float(CLIP * rows * width)
    totals = jnp.sum(stat_recv[...], axis=0) / size
    group_mean, group_sq = pool(
        jnp.where(lane < GROUPS, totals, 0.0),
        jnp.where((lane >= GROUPS) & (lane < 2 * GROUPS), totals, 0.0),
        members_t,
    )
    group_inv = lax.rsqrt(group_sq - group_mean * group_mean + EPS)
    loads[6].wait()
    loads[7].wait()
    gain = gain_ref[...].reshape(1, chans)
    bias = bias_ref[...].reshape(1, chans)
    value = (joined[...] - group_mean) * group_inv * gain + bias
    active = value / (1.0 + jnp.exp(-value))
    active = active.astype(BF16).astype(F32)

    column = lax.rem(lax.broadcasted_iota(jnp.int32, (rows, chans), 0), W)
    body_rows = slice(W, rows + W)
    window[body_rows, 0:chans] = jnp.where(column == 0, 0.0, pltpu.roll(active, 1, 0)).astype(BF16)
    window[body_rows, chans:2 * chans] = active.astype(BF16)
    window[body_rows, 2 * chans:] = jnp.where(
        column == W - 1, 0.0, pltpu.roll(active, rows - 1, 0)
    ).astype(BF16)
    loads[3].wait()
    loads[8].wait()
    ln_gain = ln_ref[...].reshape(1, chans)
    deep = rows // HALVES
    for half in range(HALVES):
        top = half * deep
        resid = joined[top:top + deep, :]
        for tap in range(3):
            start = top + tap * W
            resid = resid + jnp.dot(
                window[start:start + deep, :], conv_ref[tap], preferred_element_type=F32
            )
        joined[top:top + deep, :] = resid
        mean = jnp.mean(resid, axis=-1, keepdims=True)
        centred = resid - mean
        var = jnp.mean(centred * centred, axis=-1, keepdims=True)
        normed = centred * lax.rsqrt(var + EPS) * ln_gain
        norm_send[half * per:(half + 1) * per] = normed.reshape(
            (per,) + norm_send.shape[1:]
        ).astype(BF16)

        for step in both_ways(per):
            place = lax.rem(spot // HALVES + step, per)
            give_row(half * per + place, place * HALVES + half)
    for step in range(1, HALVES):
        half = lax.rem(spot + step, HALVES)
        place = spot // HALVES
        give_row(half * per + place, place * HALVES + half)
    norm_recv[spot] = norm_send[own_block]
    loads[4].wait()
    loads[5].wait()
    arrive(2, CLIP, norm_recv)

    pix = norm_send.shape[1]
    tokens = flat(norm_recv[...]).astype(BF16)
    qkv = jnp.dot(tokens, qkv_ref[...], preferred_element_type=F32).astype(BF16)
    same = (
        lax.rem(lax.broadcasted_iota(jnp.int32, (rows, rows), 0), pix)
        == lax.rem(lax.broadcasted_iota(jnp.int32, (rows, rows), 1), pix)
    )
    low = lax.broadcasted_iota(jnp.int32, (rows, LANES), 1) < HD
    scale = 1.0 / math.sqrt(HD)
    halves = (low, jnp.logical_not(low))
    pairs = chans // LANES
    for pair in range(pairs):
        lo = pair * LANES
        queries = qkv[:, lo:lo + LANES].astype(F32) * scale
        keys = qkv[:, chans + lo:chans + lo + LANES]
        for side, half in enumerate(halves):
            scores[2 * pair + side] = lax.dot_general(
                jnp.where(half, queries, 0.0).astype(BF16), keys, (((1,), (1,)), ((), ())),
                preferred_element_type=F32,
            )
    for head in range(2 * pairs):
        masked = jnp.where(same, scores[head], -jnp.inf)
        expon = jnp.exp(masked - jnp.max(masked, axis=-1, keepdims=True))
        weights[head] = (expon * (1.0 / jnp.sum(expon, axis=-1, keepdims=True))).astype(BF16)
    for pair in range(pairs):
        lo = pair * LANES
        values = qkv[:, 2 * chans + lo:2 * chans + lo + LANES]
        mixed = [
            jnp.dot(weights[2 * pair + side], values, preferred_element_type=F32)
            for side in range(2)
        ]
        result = jnp.where(low, mixed[0], mixed[1])
        att_send[:, :, lo:lo + LANES] = result.reshape(CLIP, pix, LANES).astype(BF16)
    att_recv[own_block] = att_send[spot]
    exchange(3, base, CLIP, spot, lambda other: att_send.at[other], att_recv, own_block)
    arrive(3, CLIP, att_recv)
    attended = flat(att_recv[...]).astype(BF16)
    out_ref[...] = (
        joined[...] + jnp.dot(attended, wout_ref[...], preferred_element_type=F32)
    ).astype(BF16)
    if fused_entry:
        leave(0, n, zero_recv)
    leave(1, CLIP, stat_recv)
    leave(2, CLIP, norm_recv)
    leave(3, CLIP, att_recv)


def body(
    skip, control, zero_weight, gn_gain, gn_bias, conv_weight, ln_gain, qkv_weight, out_weight
):
    f_dev, rows, chans = skip.shape
    n = lax.axis_size("frames")
    frames, pix_dev, _ = control.shape
    assert f_dev == 1 and n % CLIP == 0 and rows % CLIP == 0
    fused_entry = pix_dev % 8 == 0
    if fused_entry:
        entry = control.reshape(frames * pix_dev, chans)
        entry_block = (n, pix_dev, chans)
    else:
        zero_out = jnp.dot(
            control.reshape(-1, chans), zero_weight, preferred_element_type=F32
        ).astype(BF16).reshape(control.shape)
        entry = lax.all_to_all(
            zero_out, "frames", split_axis=0, concat_axis=1, tiled=True
        ).reshape(rows, chans)
        entry_block = (8, 8, LANES)
    pix = rows // CLIP
    block = (CLIP, pix, chans)
    hbm_spec = pl.BlockSpec(memory_space=pltpu.HBM)
    vmem_spec = pl.BlockSpec(memory_space=pltpu.VMEM)
    call = pl.pallas_call(
        functools.partial(kernel, n, fused_entry),
        out_shape=jax.ShapeDtypeStruct((rows, chans), BF16),
        in_specs=[hbm_spec] * 9,
        out_specs=vmem_spec,
        scratch_shapes=[
            pltpu.VMEM((rows, chans), BF16),
            pltpu.VMEM(entry.shape, BF16),
            pltpu.VMEM(zero_weight.shape, BF16),
            pltpu.VMEM((3, 3 * chans, chans), BF16),
            pltpu.VMEM(qkv_weight.shape, BF16),
            pltpu.VMEM(out_weight.shape, BF16),
            pltpu.VMEM((chans,), F32),
            pltpu.VMEM((chans,), F32),
            pltpu.VMEM((chans,), F32),
            pltpu.VMEM(entry_block, BF16),
            pltpu.VMEM(entry_block, BF16),
            pltpu.VMEM((rows, chans), F32),
            pltpu.VMEM((1, LANES), F32),
            pltpu.VMEM((CLIP, 1, LANES), F32),
            pltpu.VMEM((rows + 2 * W, 3 * chans), BF16),
            pltpu.VMEM(block, BF16),
            pltpu.VMEM(block, BF16),
            pltpu.VMEM(block, BF16),
            pltpu.VMEM(block, BF16),
            pltpu.VMEM((HEADS, rows, rows), F32),
            pltpu.VMEM((HEADS, rows, rows), BF16),
            pltpu.SemaphoreType.DMA((9,)),
            pltpu.SemaphoreType.DMA((4,)),
            pltpu.SemaphoreType.DMA((4,)),
        ],
        compiler_params=pltpu.CompilerParams(
            collective_id=0, has_side_effects=True, vmem_limit_bytes=60 * 1024 * 1024
        ),
    )
    out = call(
        skip.reshape(rows, chans), entry, zero_weight, gn_gain, gn_bias,
        conv_weight.reshape(3, 3 * chans, chans), ln_gain, qkv_weight, out_weight,
    )
    return out.reshape(skip.shape)


def solution(mesh):
    frames = P(("groups", "frames"), None, None)
    return jax.shard_map(
        body, mesh=mesh,
        in_specs=(frames, P("groups", "frames", None), P(), P(), P(), P(), P(), P(), P()),
        out_specs=frames, check_vma=False,
    )
```
